256 devices in a mesh: dp: 32 (over z_lo, y, core), tensor: 8 (over x, z_hi).
Axes of the slice: x: 4, y: 4, z: 8 (z_hi: 2, z_lo: 4; z = z_hi * 4 + z_lo), core: 2. Of those that a mesh axis runs over, the one named last changes fastest.
Arguments:
- hidden_in: bfloat16 [65536, 14336], P('dp', 'tensor'), may hold values from -6 to 6
- grad_out: bfloat16 [65536, 4096], P('dp', 'tensor'), may hold values from -6 to 6
- proj_in: bfloat16 [14336, 64], P('tensor')
- proj_out: bfloat16 [4096, 64], P('tensor')
- lengths: int32 [1024], P('dp'), may hold values from 16 to 64
- store_row: int32 [1024], replicated, may hold values from 0 to 1023, as said below
- queries: bfloat16 [1024, 4096], P('dp', 'tensor'), may hold values from -6 to 6
Outputs:
- store: bfloat16 [1024, 4096], P('dp', 'tensor')
- scores: float32 [1024, 1024], P('dp', 'tensor')
The draws below stay inside these ranges and needn't reach their ends.
Inputs may be any that keep to these rules, and one draw needn't show every extreme that they name: store_row is a permutation; the sequences of each index of dp are written to every block of 32 consecutive store rows equally often, 32 * 32 / 1024 times.
All inputs are finite; a program needn't handle non-finite values.
Results may differ from the reference program's by a relative error of at most 0.0029.
Values may be sent and summed in bfloat16 or wider, within the bound.
A program may use at most 64 MiB of HBM per device.

```python
import math
import jax
import jax.numpy as jnp
from jax import lax

D = 4096
FF = 14336
R = 64
LEN = 64
SEQ_DEV = 32
SEQS = 1024
NQ = 1024
TOKENS = 65536


def column_weights(key, rows, rise, fan_in):
    key_base, key_spread = jax.random.split(key)
    base_vals = jax.random.normal(key_base, (rows, R), jnp.float32)
    spread = jnp.exp(jax.random.uniform(key_spread, (R,), jnp.float32, 0.0, math.log(3.0)))
    column_scale = jnp.exp(rise * jnp.arange(R, dtype=jnp.float32) / (R - 1)) * spread
    return (base_vals * column_scale[None, :] / math.sqrt(fan_in)).astype(jnp.bfloat16)


def draw_proj_in(key, part):
    key = jax.random.fold_in(key, 1)
    return column_weights(key, FF, 0.55, FF)


def draw_proj_out(key, part):
    key = jax.random.fold_in(key, 2)
    return column_weights(key, D, 0.0, D)


def draw_store_row(key, part):
    key = jax.random.fold_in(key, 5)
    src_count = SEQS // SEQ_DEV
    per_pair = SEQ_DEV // src_count
    key_dest, key_slot = jax.random.split(key)
    base_dest = jnp.repeat(jnp.arange(src_count, dtype=jnp.int32), per_pair)
    dest = jax.vmap(lambda sub: jax.random.permutation(sub, base_dest))(jax.random.split(key_dest, src_count))
    onehot = (dest[:, :, None] == jnp.arange(src_count, dtype=jnp.int32)[None, None, :]).astype(jnp.int32)
    earlier = jnp.sum((jnp.cumsum(onehot, axis=1) - onehot) * onehot, axis=2)
    position = jnp.arange(src_count, dtype=jnp.int32)[:, None] * per_pair + earlier
    slot_perms = jax.vmap(lambda sub: jax.random.permutation(sub, SEQ_DEV))(jax.random.split(key_slot, src_count)).astype(jnp.int32)
    local_slot = slot_perms[dest, position]
    return (dest * SEQ_DEV + local_slot).reshape(SEQS).astype(jnp.int32)


def set_ends(entries, own_key, low, high):
    longest = entries.shape.index(max(entries.shape))
    spots = []
    for shift in (0, 1):
        where = [jax.random.randint(jax.random.fold_in(own_key, axis), (), 0, length) for axis, length in enumerate(entries.shape)]
        where[longest] = (where[longest] + shift) % entries.shape[longest]
        spots.append(tuple(where))
    return entries.at[spots[0]].set(low).at[spots[1]].set(high)


def levels(key, extent, shards, least, high):
    level, own = 1.0, jax.random.fold_in(key, 6)
    for axis_at, blocks in shards:
        heights = jnp.exp(jax.random.uniform(jax.random.fold_in(own, axis_at), (blocks,), jnp.float32, least / len(shards), high / len(shards)))
        level = level * jnp.repeat(heights, extent[axis_at] // blocks).reshape([-1 if axis == axis_at else 1 for axis in range(len(extent))])
    return level


def gaussian(key, extent, deviation, bound, cuts=(), kind=jnp.bfloat16):
    factor_of = levels(key, extent, cuts, -0.22, 0.18) if cuts else 1.0
    drawn = jax.random.normal(key, extent, jnp.float32) * deviation * factor_of
    return jnp.minimum(jnp.maximum(drawn, -bound), bound).astype(kind)


def setup_inputs(seed: int = 0) -> dict:
    key_list = jax.random.split(jax.random.key(seed), 8)
    hidden_in = gaussian(key_list[0], (TOKENS, FF), 1.0, 6.0, ((0, 32), (1, 8)))
    grad_out = gaussian(key_list[1], (TOKENS, D), 1.0, 6.0, ((0, 32), (1, 8)))
    proj_in = draw_proj_in(jax.random.fold_in(key_list[7], 71), 0)
    proj_out = draw_proj_out(jax.random.fold_in(key_list[7], 71), 0)
    lengths = set_ends(jax.random.randint(key_list[4], (SEQS,), LEN // 4, LEN + 1), jax.random.fold_in(key_list[4], 1), LEN // 4, LEN).astype(jnp.int32)
    store_row = draw_store_row(jax.random.fold_in(key_list[7], 71), 0)
    queries = gaussian(key_list[6], (NQ, R * R), 1.0, 6.0, ((0, 32), (1, 8)))
    return dict(hidden_in=hidden_in, grad_out=grad_out, proj_in=proj_in, proj_out=proj_out, lengths=lengths, store_row=store_row, queries=queries)


def outer_sums(left_fac, right_fac, seq_lengths):
    seq_count = seq_lengths.shape[0]
    positions = jnp.arange(LEN, dtype=jnp.int32)
    live_mask = (positions[None, :] < seq_lengths[:, None]).astype(jnp.float32)
    left_blocks = left_fac.reshape(seq_count, LEN, -1) * live_mask[:, :, None]
    right_blocks = right_fac.reshape(seq_count, LEN, -1)
    kron = jnp.einsum('sti,stj->sij', left_blocks, right_blocks, precision=lax.Precision.HIGHEST)
    return kron.reshape(seq_count, -1)

def reference(hidden_in, grad_out, proj_in, proj_out, lengths, store_row, queries):
    in_fac = jnp.dot(hidden_in, proj_in, preferred_element_type=jnp.float32)
    out_fac = jnp.dot(grad_out, proj_out, preferred_element_type=jnp.float32)
    kron = outer_sums(in_fac, out_fac, lengths)
    inv_norm = 1.0 / jnp.sqrt(lax.optimization_barrier(jnp.mean(kron * kron, axis=1)) + 1e-06)
    normed = (kron * inv_norm[:, None]).astype(jnp.bfloat16)
    store = jnp.zeros((SEQS, R * R), jnp.bfloat16).at[store_row].set(normed)
    scores = jnp.dot(store, queries.T, preferred_element_type=jnp.float32) / R
    return (store, scores)
```

```python
import jax
import jax.numpy as jnp
from jax import lax
from jax.experimental import pallas as pl
from jax.experimental.pallas import tpu as pltpu
from jax.sharding import PartitionSpec as P

MESH = pl.DeviceIdType.MESH
DP, TP = 32, 8
NX, NY, NZ = 4, 4, 4
SEQ, LEN, R = 32, 64, 64
STEPS = 4
CHUNKS = 8
QROWS, QCOLS = 32, 512
TOP = 32767.0


def quantize(block):
    peak = jnp.maximum(jnp.max(jnp.abs(block), axis=0, keepdims=True), 1e-30)
    values = jnp.round(block * (TOP / peak)).astype(jnp.int32).astype(jnp.int16)
    return values, peak * (1.0 / TOP)


def dequantize(values, scale):
    return values.astype(jnp.int32).astype(jnp.float32) * scale


def kernel(
    hid, grad, win, wout, lens_in, rows_in, queries, store_ref, scores_ref,
    hid_v, grad_v, win_v, wout_v, wide_in, wide_out, lens_v, rows_v, sigma_v, sigma_s,
    part, coded, scale, xsend, xsscale, xrecv, xrscale, own, zsend, zsscale, zrecv, zrscale,
    bsend, brecv, qall, flat, wide,
    load_sem, hid_sem, grad_sem, sig_sem, xs_sem, xr_sem, xcs_sem, xcr_sem,
    zs_sem, zr_sem, zcs_sem, zcr_sem, bs_sem, br_sem, qs_sem, qr_sem,
):
    dp, tn = lax.axis_index("dp"), lax.axis_index("tensor")
    zl, y, core = dp // 8, (dp // 2) % 4, dp % 2
    x, zh = tn // 2, tn % 2
    shift = dp % STEPS

    def remote(src, dst, send, recv, device):
        return pltpu.make_async_remote_copy(
            src_ref=src, dst_ref=dst, send_sem=send, recv_sem=recv, device_id=device, device_id_type=MESH
        )

    loads = [
        pltpu.make_async_copy(src, dst, load_sem.at[i])
        for i, (src, dst) in enumerate(
            [(rows_in, rows_v), (lens_in, lens_v), (win, win_v), (wout, wout_v)]
        )
    ]
    for load in loads:
        load.start()
    tokens = hid_v.shape[0] // CHUNKS
    chunk_loads = []
    for i in range(CHUNKS):
        at = pl.ds(i * tokens, tokens)
        pair = (
            pltpu.make_async_copy(hid.at[at], hid_v.at[at], hid_sem.at[i]),
            pltpu.make_async_copy(grad.at[at], grad_v.at[at], grad_sem.at[i]),
        )
        for load in pair:
            load.start()
        chunk_loads.append(pair)

    x_peers = [(dp, lax.rem(x + d, NX) * 2 + zh) for d in (1, 2, 3)]
    z_peer = (dp, x * 2 + 1 - zh)
    zl_peers = [(lax.rem(zl + d, NZ) * 8 + y * 2 + core, tn) for d in (1, 2, 3)]
    y_peers = [(zl * 8 + lax.rem(y + d, NY) * 2 + core, tn) for d in (1, 2, 3)]
    core_peer = (zl * 8 + y * 2 + 1 - core, tn)
    q_target = (x * 8 + ((y % 2) * 2 + zh) * 2 + 1 - core, zl * 2 + y // 2)
    q_source = (x * 8 + (zh * 2 + y // 2) * 2 + 1 - core, zl * 2 + y % 2)
    self_row = tn == dp // STEPS
    barrier = pltpu.get_barrier_semaphore()

    def greet(device):
        pl.semaphore_signal(barrier, inc=1, device_id=device, device_id_type=MESH)

    for device in [*x_peers, z_peer, *zl_peers, *y_peers, core_peer, q_source]:
        greet(device)
    for d in range(1, DP):
        greet((lax.rem(dp + d, DP), dp // STEPS))

    @pl.when(jnp.logical_not(self_row))
    def _():
        greet((dp, dp // STEPS))

    loads[0].wait()
    targets = lax.shift_right_logical(rows_v[pl.ds(dp, 1), :], 5)
    block_of = lax.broadcasted_iota(jnp.int32, (DP, SEQ), 0)
    seq_of = lax.broadcasted_iota(jnp.int32, (DP, SEQ), 1)
    sigma = jnp.sum(jnp.where(targets == block_of, seq_of, 0), axis=1, keepdims=True)
    sigma_v[...] = jnp.broadcast_to(jnp.minimum(sigma, SEQ - 1), sigma_v.shape)
    sig_copy = pltpu.make_async_copy(sigma_v, sigma_s, sig_sem)
    sig_copy.start()
    loads[1].wait()
    for load in loads[2:]:
        load.wait()
    zero_in = jnp.zeros_like(win_v)
    wide_in[...] = jnp.concatenate([win_v[...], zero_in], axis=1)
    zero_out = jnp.zeros_like(wout_v)
    wide_out[...] = jnp.concatenate([zero_out, wout_v[...]], axis=1)

    pl.semaphore_wait(barrier, DP + 12 - self_row.astype(jnp.int32))

    slot1 = x * 8 + ((y % 2) * 2 + zh) * 2 + 1 - core
    q_copies = [remote(queries, qall.at[slot1], qs_sem.at[0], qr_sem.at[0], q_target)]
    q_copies[0].start()

    position = lax.broadcasted_iota(jnp.int32, (LEN, 2 * R), 0)
    for i in range(CHUNKS):
        at = pl.ds(i * tokens, tokens)
        for load in chunk_loads[i]:
            load.wait()
        out = jnp.dot(hid_v[at, :], wide_in[...], preferred_element_type=jnp.float32)
        out += jnp.dot(grad_v[at, :], wide_out[...], preferred_element_type=jnp.float32)
        for j in range(tokens // LEN):
            s = i * (tokens // LEN) + j
            block = jnp.where(position < lens_v[s : s + 1, :], out[j * LEN : (j + 1) * LEN], 0.0)
            part[s] = block
            coded[s], scale[s : s + 1, :] = quantize(block)
        if i == 2:
            q_copies[0].wait_recv()
            mine = qall.at[dp]
            for d, device in enumerate(zl_peers):
                q_copies.append(remote(mine, mine, qs_sem.at[1 + d], qr_sem.at[1 + d], device))
                q_copies[-1].start()
        if i == 6:
            for copy in q_copies[1:4]:
                copy.wait_recv()
            for d, device in enumerate(y_peers):
                for z in range(NZ):
                    block = qall.at[z * 8 + y * 2 + core]
                    n = 4 + d * NZ + z
                    q_copies.append(remote(block, block, qs_sem.at[n], qr_sem.at[n], device))
                    q_copies[-1].start()

    sig_copy.wait()

    def source(k, tensor):
        return sigma_s[tensor * STEPS + lax.rem(k + shift, STEPS), 0]

    x_copies, xc_copies = {}, []
    for d in (2, 1, 3):
        for k in range(STEPS):
            for h in range(2):
                s = source(k, lax.rem(x + d, NX) * 2 + h)
                xsscale[d - 1, 2 * k + h : 2 * k + h + 1, :] = scale[pl.ds(s, 1), :]
        copy = remote(xsscale.at[d - 1], xrscale.at[d - 1], xcs_sem.at[d - 1], xcr_sem.at[d - 1], x_peers[d - 1])
        copy.start()
        xc_copies.append(copy)
    for k in range(STEPS):
        for d in (2, 1, 3):
            for h in range(2):
                xsend[d - 1, k, h] = coded[source(k, lax.rem(x + d, NX) * 2 + h)]
            n = (d - 1) * STEPS + k
            copy = remote(xsend.at[d - 1, k], xrecv.at[d - 1, k], xs_sem.at[n], xr_sem.at[n], x_peers[d - 1])
            copy.start()
            x_copies[k, d] = copy

    for copy in q_copies[4:]:
        copy.wait_recv()
    for z in range(NZ):
        for yy in range(NY):
            block = qall.at[z * 8 + yy * 2 + core]
            n = 16 + z * NY + yy
            q_copies.append(remote(block, block, qs_sem.at[n], qr_sem.at[n], core_peer))
            q_copies[-1].start()

    for copy in xc_copies:
        copy.wait_recv()
    z_copies, zc_copies, b_copies = [], [], []

    def x_sum(k, h):
        total = part[source(k, x * 2 + h)]
        for d in (1, 2, 3):
            total += dequantize(xrecv[d - 1, k, h], xrscale[d - 1, pl.ds(2 * k + h, 1), :])
        return total

    def z_step(k):
        for d in (2, 1, 3):
            x_copies[k, d].wait_recv()
        zsend[k], zsscale[k] = quantize(x_sum(k, 1 - zh))
        z_copies.append(remote(zsend.at[k], zrecv.at[k], zs_sem.at[k], zr_sem.at[k], z_peer))
        z_copies[-1].start()
        zc_copies.append(remote(zsscale.at[k], zrscale.at[k], zcs_sem.at[k], zcr_sem.at[k], z_peer))
        zc_copies[-1].start()
        own[k] = x_sum(k, zh)

    def b_step(k):
        z_copies[k].wait_recv()
        zc_copies[k].wait_recv()
        total = own[k] + dequantize(zrecv[k], zrscale[k])
        kron = lax.dot_general(
            total[:, :R], total[:, R:], (((0,), (0,)), ((), ())),
            precision=lax.Precision.HIGHEST, preferred_element_type=jnp.float32,
        )
        mean = jnp.sum(jnp.sum(kron * kron, axis=0, keepdims=True), axis=1, keepdims=True) * (1.0 / (R * R))
        normed = kron * (1.0 / jnp.sqrt(mean + 1e-06))
        bsend[k] = normed.reshape(R * R // 128, 128).astype(jnp.bfloat16)
        q = tn * STEPS + lax.rem(k + shift, STEPS)
        for d in range(TP):
            copy = remote(bsend.at[k], brecv.at[dp], bs_sem.at[k * TP + d], br_sem, (q, lax.rem(tn + d, TP)))
            if k == 0 and d == 0:

                @pl.when(self_row)
                def _():
                    pltpu.make_async_copy(bsend.at[k], brecv.at[dp], br_sem).start()

                @pl.when(jnp.logical_not(self_row))
                def _(copy=copy):
                    copy.start()
            else:
                copy.start()
            b_copies.append(copy)

    z_step(0)
    for k in range(1, STEPS):
        z_step(k)
        b_step(k - 1)
    b_step(STEPS - 1)

    rows = rows_v[...]
    slot = jnp.sum(
        jnp.where(lax.shift_right_logical(rows, 5) == dp, lax.bitwise_and(rows, 31), 0), axis=1, keepdims=True
    )
    place = lax.broadcasted_iota(jnp.int32, (DP, SEQ), 1) == slot
    for copy in q_copies[16:]:
        copy.wait_recv()

    pltpu.make_async_copy(brecv, brecv, br_sem).wait()
    flat[...] = brecv[...].reshape(flat.shape).astype(jnp.float32)
    cols = R * R // 128
    for a in range(cols):
        wide[:, a * 128 : (a + 1) * 128] = flat[pl.ds(a, DP, stride=cols), :].astype(jnp.bfloat16)
    ordered = place.astype(jnp.bfloat16)
    mine = wide[:, pl.ds(pl.multiple_of(tn * QCOLS, QCOLS), QCOLS)]
    store_ref[...] = lax.dot_general(
        ordered, mine, (((0,), (0,)), ((), ())), preferred_element_type=jnp.float32
    ).astype(jnp.bfloat16)
    total = jnp.zeros((DP, 4 * QROWS), jnp.float32)
    for c in range(TP):
        block = jnp.concatenate(
            [qall[(c // 2) * 8 + ((m // 2) * 2 + c % 2) * 2 + 1 - m % 2] for m in range(4)], axis=0
        )
        total += lax.dot_general(
            wide[:, c * QCOLS : (c + 1) * QCOLS], block, (((1,), (1,)), ((), ())), preferred_element_type=jnp.float32
        )
    scores_ref[...] = lax.dot_general(
        place.astype(jnp.float32), total, (((0,), (0,)), ((), ())),
        precision=lax.Precision.HIGHEST, preferred_element_type=jnp.float32,
    ) * (1.0 / R)

    for copy in [*q_copies, *xc_copies, *x_copies.values(), *z_copies, *zc_copies, *b_copies[1:]]:
        copy.wait_send()

    @pl.when(jnp.logical_not(self_row))
    def _():
        b_copies[0].wait_send()


def per_device(hidden_in, grad_out, proj_in, proj_out, lengths, store_row, queries):
    lens = jnp.broadcast_to(lengths[:, None], (SEQ, 2 * R))
    rows = store_row.reshape(DP, SEQ)
    dma, vmem = pltpu.SemaphoreType.DMA, pltpu.VMEM
    bf16, f32, i16, i32 = jnp.bfloat16, jnp.float32, jnp.int16, jnp.int32
    tokens, wide_k = hidden_in.shape
    narrow_k = grad_out.shape[1]
    return pl.pallas_call(
        kernel,
        out_shape=(
            jax.ShapeDtypeStruct((SEQ, QCOLS), bf16),
            jax.ShapeDtypeStruct((SEQ, 4 * QROWS), f32),
        ),
        in_specs=[pl.BlockSpec(memory_space=pl.ANY)] * 7,
        out_specs=(pl.BlockSpec(memory_space=pltpu.VMEM),) * 2,
        scratch_shapes=[
            vmem((tokens, wide_k), bf16), vmem((tokens, narrow_k), bf16),
            vmem((wide_k, R), bf16), vmem((narrow_k, R), bf16),
            vmem((wide_k, 2 * R), bf16), vmem((narrow_k, 2 * R), bf16),
            vmem((SEQ, 2 * R), i32), vmem((DP, SEQ), i32),
            vmem((DP, 128), i32), pltpu.SMEM((DP, 128), i32),
            vmem((SEQ, LEN, 2 * R), f32), vmem((SEQ, LEN, 2 * R), i16), vmem((SEQ, 2 * R), f32),
            vmem((3, STEPS, 2, LEN, 2 * R), i16), vmem((3, 2 * STEPS, 2 * R), f32),
            vmem((3, STEPS, 2, LEN, 2 * R), i16), vmem((3, 2 * STEPS, 2 * R), f32),
            vmem((STEPS, LEN, 2 * R), f32),
            vmem((STEPS, LEN, 2 * R), i16), vmem((STEPS, 1, 2 * R), f32),
            vmem((STEPS, LEN, 2 * R), i16), vmem((STEPS, 1, 2 * R), f32),
            vmem((STEPS, 32, 128), bf16), vmem((DP, 32, 128), bf16),
            vmem((DP, QROWS, QCOLS), bf16), vmem((DP * 32, 128), f32), vmem((DP, R * R), bf16),
            dma((4,)), dma((CHUNKS,)), dma((CHUNKS,)), dma,
            dma((3 * STEPS,)), dma((3 * STEPS,)), dma((3,)), dma((3,)),
            dma((STEPS,)), dma((STEPS,)), dma((STEPS,)), dma((STEPS,)),
            dma((STEPS * TP,)), dma, dma((32,)), dma((32,)),
        ],
        compiler_params=pltpu.CompilerParams(collective_id=0, has_side_effects=True, vmem_limit_bytes=48 * 2**20),
    )(hidden_in, grad_out, proj_in, proj_out, lens, rows, queries)


def solution(mesh):
    placed = (
        P("dp", "tensor"), P("dp", "tensor"), P("tensor", None), P("tensor", None),
        P("dp"), P(), P("dp", "tensor"),
    )
    return jax.shard_map(
        per_device, mesh=mesh, in_specs=placed, out_specs=(P("dp", "tensor"), P("dp", "tensor")), check_vma=False
    )
```

```python
import jax
import jax.numpy as jnp
from jax import lax
from jax.experimental import pallas as pl
from jax.experimental.pallas import tpu as pltpu
from jax.sharding import PartitionSpec as P

MESH = pl.DeviceIdType.MESH
DP, TP = 32, 8
NX, NY, NZ = 4, 4, 4
SEQ, LEN, R = 32, 64, 64
STEPS = 4
CHUNKS = 8
AHEAD = 3
GREET = 3
QROWS, QCOLS = 32, 512
TOP = 32767.0


def quantize(block):
    peak = jnp.maximum(jnp.max(jnp.abs(block), axis=0, keepdims=True), 1e-30)
    values = jnp.round(block * (TOP / peak)).astype(jnp.int32).astype(jnp.int16)
    return values, peak * (1.0 / TOP)


def dequantize(values, scale):
    return values.astype(jnp.int32).astype(jnp.float32) * scale


def kernel(
    hid, grad, win, wout, lens_in, rows_in, queries, store_ref, scores_ref,
    hid_v, grad_v, win_v, wout_v, wide_in, wide_out, lens_s, rows_v, sigma_v, sigma_s,
    part, coded, scale, xsend, xsscale, xrecv, xrscale, own, zsend, zsscale, zrecv, zrscale,
    bsend, brecv, qall, flat, wide,
    load_sem, hid_sem, grad_sem, sig_sem, xs_sem, xr_sem, xcs_sem, xcr_sem,
    zs_sem, zr_sem, zcs_sem, zcr_sem, bs_sem, br_sem, qs_sem, qr_sem, known_sem,
):
    dp, tn = lax.axis_index("dp"), lax.axis_index("tensor")
    zl, y, core = dp // 8, (dp // 2) % 4, dp % 2
    x, zh = tn // 2, tn % 2
    shift = dp % STEPS

    def remote(src, dst, send, recv, device):
        return pltpu.make_async_remote_copy(
            src_ref=src, dst_ref=dst, send_sem=send, recv_sem=recv, device_id=device, device_id_type=MESH
        )

    loads = [
        pltpu.make_async_copy(src, dst, load_sem.at[i])
        for i, (src, dst) in enumerate(
            [(rows_in, rows_v), (lens_in, lens_s), (win, win_v), (wout, wout_v)]
        )
    ]
    for load in loads:
        load.start()
    tokens = hid_v.shape[0] // CHUNKS
    chunk_loads = []
    for i in range(CHUNKS):
        at = pl.ds(i * tokens, tokens)
        chunk_loads.append((
            pltpu.make_async_copy(hid.at[at], hid_v.at[at], hid_sem.at[i]),
            pltpu.make_async_copy(grad.at[at], grad_v.at[at], grad_sem.at[i]),
        ))
    for pair in chunk_loads[:AHEAD]:
        for load in pair:
            load.start()

    x_peers = [(dp, lax.rem(x + d, NX) * 2 + zh) for d in (1, 2, 3)]
    z_peer = (dp, x * 2 + 1 - zh)
    y_peers = [(zl * 8 + lax.rem(y + d, NY) * 2 + core, tn) for d in (1, 2, 3)]
    core_peer = (zl * 8 + y * 2 + 1 - core, tn)
    q_y = (y % 2) * 2 + zh
    q_targets = [(z * 8 + q_y * 2 + 1 - core, zl * 2 + y // 2) for z in range(NZ)]
    q_sources = [(x * 8 + (zh * 2 + y // 2) * 2 + 1 - core, z * 2 + y % 2) for z in range(NX)]
    self_row = tn == dp // STEPS
    barrier = pltpu.get_barrier_semaphore()

    def signal(sem, devices):
        for device in devices:
            pl.semaphore_signal(sem, inc=1, device_id=device, device_id_type=MESH)

    signal(barrier, [*q_sources, z_peer, *x_peers, *y_peers, core_peer])

    loads[0].wait()
    rows = rows_v[...]
    flat_at = lax.broadcasted_iota(jnp.int32, rows.shape, 0) * 128 + lax.broadcasted_iota(jnp.int32, rows.shape, 1)
    holder, seq_of = lax.shift_right_logical(flat_at, 5), lax.bitwise_and(flat_at, 31)
    block_of, place_of = lax.shift_right_logical(rows, 5), lax.bitwise_and(rows, 31)
    block_of = jnp.where(holder == dp, block_of, -1)
    each = lax.broadcasted_iota(jnp.int32, (DP, *rows.shape), 0)
    sigma = jnp.sum(jnp.where(block_of[None] == each, seq_of[None], 0), axis=1)
    sigma = jnp.sum(sigma, axis=1, keepdims=True)
    sigma_v[...] = jnp.broadcast_to(jnp.minimum(sigma, SEQ - 1), sigma_v.shape)
    sig_copy = pltpu.make_async_copy(sigma_v, sigma_s, sig_sem)
    sig_copy.start()
    loads[1].wait()
    for load in loads[2:]:
        load.wait()
    wide_in[...] = jnp.concatenate([win_v[...], jnp.zeros_like(win_v)], axis=0).T
    wide_out[...] = jnp.concatenate([jnp.zeros_like(wout_v), wout_v[...]], axis=0).T

    q_copies = []
    position = lax.broadcasted_iota(jnp.int32, (LEN, 2 * R), 0)
    for i in range(CHUNKS):
        at = pl.ds(i * tokens, tokens)
        for load in chunk_loads[i]:
            load.wait()
        if i + AHEAD < CHUNKS:
            for load in chunk_loads[i + AHEAD]:
                load.start()
        out = jnp.dot(hid_v[at, :], wide_in[...], preferred_element_type=jnp.float32)
        out += jnp.dot(grad_v[at, :], wide_out[...], preferred_element_type=jnp.float32)
        for j in range(tokens // LEN):
            s = i * (tokens // LEN) + j
            block = jnp.where(position < lens_s[s], out[j * LEN : (j + 1) * LEN], 0.0)
            part[s] = block
            coded[s], scale[s : s + 1, :] = quantize(block)
        if i == GREET:
            pl.semaphore_wait(barrier, 12)
            for z, device in enumerate(q_targets):
                q_copies.append(
                    remote(queries, qall.at[1 - core, q_y, x], qs_sem.at[z], qr_sem.at[x], device)
                )
                q_copies[-1].start()

    sig_copy.wait()

    def source(k, tensor):
        return sigma_s[tensor * STEPS + lax.rem(k + shift, STEPS), 0]

    x_copies, xc_copies = {}, []
    for d in (2, 1, 3):
        for k in range(STEPS):
            for h in range(2):
                s = source(k, lax.rem(x + d, NX) * 2 + h)
                xsscale[d - 1, 2 * k + h : 2 * k + h + 1, :] = scale[pl.ds(s, 1), :]
        copy = remote(xsscale.at[d - 1], xrscale.at[d - 1], xcs_sem.at[d - 1], xcr_sem.at[d - 1], x_peers[d - 1])
        copy.start()
        xc_copies.append(copy)
    for k in range(STEPS):
        for d in (2, 1, 3):
            for h in range(2):
                xsend[d - 1, k, h] = coded[source(k, lax.rem(x + d, NX) * 2 + h)]
            n = (d - 1) * STEPS + k
            copy = remote(xsend.at[d - 1, k], xrecv.at[d - 1, k], xs_sem.at[n], xr_sem.at[n], x_peers[d - 1])
            copy.start()
            x_copies[k, d] = copy

    for copy in xc_copies:
        copy.wait_recv()
    z_copies, zc_copies, b_copies = [], [], []

    def x_sum(k, h):
        total = part[source(k, x * 2 + h)]
        for d in (1, 2, 3):
            total += dequantize(xrecv[d - 1, k, h], xrscale[d - 1, pl.ds(2 * k + h, 1), :])
        return total

    def z_step(k):
        for d in (2, 1, 3):
            x_copies[k, d].wait_recv()
        zsend[k], zsscale[k] = quantize(x_sum(k, 1 - zh))
        z_copies.append(remote(zsend.at[k], zrecv.at[k], zs_sem.at[k], zr_sem.at[k], z_peer))
        z_copies[-1].start()
        zc_copies.append(remote(zsscale.at[k], zrscale.at[k], zcs_sem.at[k], zcr_sem.at[k], z_peer))
        zc_copies[-1].start()
        own[k] = x_sum(k, zh)

    def b_step(k):
        z_copies[k].wait_recv()
        zc_copies[k].wait_recv()
        total = own[k] + dequantize(zrecv[k], zrscale[k])
        kron = lax.dot_general(
            total[:, :R], total[:, R:], (((0,), (0,)), ((), ())),
            precision=lax.Precision.HIGHEST, preferred_element_type=jnp.float32,
        )
        mean = jnp.sum(jnp.sum(kron * kron, axis=0, keepdims=True), axis=1, keepdims=True) * (1.0 / (R * R))
        normed = kron * (1.0 / jnp.sqrt(mean + 1e-06))
        bsend[k] = normed.reshape(R * R // 128, 128).astype(jnp.bfloat16)
        q = tn * STEPS + lax.rem(k + shift, STEPS)
        for d in range(TP):
            copy = remote(bsend.at[k], brecv.at[dp], bs_sem.at[k * TP + d], br_sem, (q, lax.rem(tn + d, TP)))
            if k == 0 and d == 0:

                @pl.when(self_row)
                def _():
                    pltpu.make_async_copy(bsend.at[k], brecv.at[dp], br_sem).start()

                @pl.when(jnp.logical_not(self_row))
                def _(copy=copy):
                    copy.start()
            else:
                copy.start()
            b_copies.append(copy)

    z_step(0)
    z_step(1)
    mine = qall.at[core, y]
    for i in range(NX):
        pltpu.make_async_copy(queries, mine.at[i], qr_sem.at[i]).wait()
    for d, device in enumerate(y_peers):
        q_copies.append(remote(mine, mine, qs_sem.at[4 + d], qr_sem.at[4 + d], device))
        q_copies[-1].start()
    signal(known_sem.at[0], y_peers)
    z_step(2)
    z_step(3)
    pl.semaphore_wait(known_sem.at[0], 3)
    signal(known_sem.at[1], [core_peer])
    pl.semaphore_wait(known_sem.at[1], 1)
    for k in range(STEPS):
        b_step(k)
    for copy in q_copies[4:]:
        copy.wait_recv()
    mine = qall.at[core]
    q_copies.append(remote(mine, mine, qs_sem.at[7], qr_sem.at[7], core_peer))
    q_copies[-1].start()

    stored_here = jnp.where(lax.shift_right_logical(rows, 5) == dp, place_of, 0)
    slot = jnp.sum(jnp.where(holder[None] == each, stored_here[None], 0), axis=1)
    slot = jnp.sum(slot, axis=1, keepdims=True)
    place = lax.broadcasted_iota(jnp.int32, (DP, SEQ), 1) == slot
    q_copies[-1].wait_recv()

    pltpu.make_async_copy(brecv, brecv, br_sem).wait()
    flat[...] = brecv[...].reshape(flat.shape).astype(jnp.float32)
    cols = R * R // 128
    for a in range(cols):
        wide[:, a * 128 : (a + 1) * 128] = flat[pl.ds(a, DP, stride=cols), :].astype(jnp.bfloat16)
    ordered = place.astype(jnp.bfloat16)
    mine = wide[:, pl.ds(pl.multiple_of(tn * QCOLS, QCOLS), QCOLS)]
    store_ref[...] = lax.dot_general(
        ordered, mine, (((0,), (0,)), ((), ())), preferred_element_type=jnp.float32
    ).astype(jnp.bfloat16)
    total = jnp.zeros((DP, 4 * QROWS), jnp.float32)
    for c in range(TP):
        block = jnp.concatenate(
            [qall[1 - m % 2, (m // 2) * 2 + c % 2, c // 2] for m in range(4)], axis=0
        )
        total += lax.dot_general(
            wide[:, c * QCOLS : (c + 1) * QCOLS], block, (((1,), (1,)), ((), ())), preferred_element_type=jnp.float32
        )
    scores_ref[...] = lax.dot_general(
        place.astype(jnp.float32), total, (((0,), (0,)), ((), ())),
        precision=lax.Precision.HIGHEST, preferred_element_type=jnp.float32,
    ) * (1.0 / R)

    for copy in [*q_copies, *xc_copies, *x_copies.values(), *z_copies, *zc_copies, *b_copies[1:]]:
        copy.wait_send()

    @pl.when(jnp.logical_not(self_row))
    def _():
        b_copies[0].wait_send()


def per_device(hidden_in, grad_out, proj_in, proj_out, lengths, store_row, queries):
    rows = store_row.reshape(-1, 128)
    dma, vmem = pltpu.SemaphoreType.DMA, pltpu.VMEM
    bf16, f32, i16, i32 = jnp.bfloat16, jnp.float32, jnp.int16, jnp.int32
    tokens, wide_k = hidden_in.shape
    narrow_k = grad_out.shape[1]
    return pl.pallas_call(
        kernel,
        out_shape=(
            jax.ShapeDtypeStruct((SEQ, QCOLS), bf16),
            jax.ShapeDtypeStruct((SEQ, 4 * QROWS), f32),
        ),
        in_specs=[pl.BlockSpec(memory_space=pltpu.HBM)] * 7,
        out_specs=(pl.BlockSpec(memory_space=pltpu.VMEM),) * 2,
        scratch_shapes=[
            vmem((tokens, wide_k), bf16), vmem((tokens, narrow_k), bf16),
            vmem((R, wide_k), bf16), vmem((R, narrow_k), bf16),
            vmem((wide_k, 2 * R), bf16), vmem((narrow_k, 2 * R), bf16),
            pltpu.SMEM((SEQ,), i32), vmem(rows.shape, i32),
            vmem((DP, 128), i32), pltpu.SMEM((DP, 128), i32),
            vmem((SEQ, LEN, 2 * R), f32), vmem((SEQ, LEN, 2 * R), i16), vmem((SEQ, 2 * R), f32),
            vmem((3, STEPS, 2, LEN, 2 * R), i16), vmem((3, 2 * STEPS, 2 * R), f32),
            vmem((3, STEPS, 2, LEN, 2 * R), i16), vmem((3, 2 * STEPS, 2 * R), f32),
            vmem((STEPS, LEN, 2 * R), f32),
            vmem((STEPS, LEN, 2 * R), i16), vmem((STEPS, 1, 2 * R), f32),
            vmem((STEPS, LEN, 2 * R), i16), vmem((STEPS, 1, 2 * R), f32),
            vmem((STEPS, 32, 128), bf16), vmem((DP, 32, 128), bf16),
            vmem((2, NY, NX, QROWS, QCOLS), bf16), vmem((DP * 32, 128), f32), vmem((DP, R * R), bf16),
            dma((4,)), dma((CHUNKS,)), dma((CHUNKS,)), dma,
            dma((3 * STEPS,)), dma((3 * STEPS,)), dma((3,)), dma((3,)),
            dma((STEPS,)), dma((STEPS,)), dma((STEPS,)), dma((STEPS,)),
            dma((STEPS * TP,)), dma, dma((8,)), dma((8,)), pltpu.SemaphoreType.REGULAR((2,)),
        ],
        compiler_params=pltpu.CompilerParams(collective_id=0, has_side_effects=True, vmem_limit_bytes=63 * 2**20),
    )(hidden_in, grad_out, proj_in.T, proj_out.T, lengths, rows, queries)


def solution(mesh):
    placed = (
        P("dp", "tensor"), P("dp", "tensor"), P("tensor", None), P("tensor", None),
        P("dp"), P(), P("dp", "tensor"),
    )
    return jax.shard_map(
        per_device, mesh=mesh, in_specs=placed, out_specs=(P("dp", "tensor"), P("dp", "tensor")), check_vma=False
    )
```

```python
import jax
import jax.numpy as jnp
from jax import lax
from jax.experimental import pallas as pl
from jax.experimental.pallas import tpu as pltpu
from jax.sharding import PartitionSpec as P

MESH = pl.DeviceIdType.MESH
DP, TP = 32, 8
NX, NY, NZ = 4, 4, 4
SEQ, LEN, R = 32, 64, 64
STEPS = 4
CHUNKS = 8
AHEAD = 4
GREET = 1
QROWS, QCOLS = 32, 512
TOP = 32767.0


def quantize(block):
    peak = jnp.maximum(jnp.max(jnp.abs(block), axis=0, keepdims=True), 1e-30)
    values = jnp.round(block * (TOP / peak)).astype(jnp.int32).astype(jnp.int16)
    return values, peak * (1.0 / TOP)


def dequantize(values, scale):
    return values.astype(jnp.int32).astype(jnp.float32) * scale


def crossed(a, b):
    return ((a - b == 3) | (b - a == 3)).astype(jnp.int32)


def tables(rows):
    at = lax.broadcasted_iota(jnp.int32, rows.shape, 0) * 128 + lax.broadcasted_iota(jnp.int32, rows.shape, 1)
    high, low = lambda v: lax.shift_right_logical(v, 5), lambda v: lax.bitwise_and(v, 31)
    return high(at), low(at), high(rows), low(rows)


def pick(keys, values, mask):
    keys = jnp.where(mask, keys, -1)
    each = lax.broadcasted_iota(jnp.int32, (DP, *keys.shape), 0)
    found = jnp.sum(jnp.where(keys[None] == each, values[None], 0), axis=1)
    return jnp.sum(found, axis=1, keepdims=True)


def own_order(rows, dp):
    holder, number, block, _ = tables(rows)
    return jnp.minimum(pick(block, number, holder == dp), SEQ - 1)


def kernel(
    hid, grad, win, wout, lens_in, rows_in, queries, store_ref, scores_ref,
    hid_v, grad_v, win_v, wout_v, wide_in, wide_out, lens_s, rows_v, sigma_v, sigma_s,
    part, coded, scale, xsend, xsscale, xrecv, xrscale, zsend, zsscale, zrecv, zrscale,
    bsend, brecv, qall, flat, wide,
    load_sem, hid_sem, grad_sem, sig_sem, xs_sem, xr_sem, xcs_sem, xcr_sem,
    zs_sem, zr_sem, zcs_sem, zcr_sem, bs_sem, br_sem, qs_sem, qr_sem, known_sem,
):
    dp, tn = lax.axis_index("dp"), lax.axis_index("tensor")
    zl, y, core = dp // 8, (dp // 2) % 4, dp % 2
    x, zh = tn // 2, tn % 2

    def remote(src, dst, send, recv, device):
        return pltpu.make_async_remote_copy(
            src_ref=src, dst_ref=dst, send_sem=send, recv_sem=recv, device_id=device, device_id_type=MESH
        )

    loads = [
        pltpu.make_async_copy(src, dst, load_sem.at[i])
        for i, (src, dst) in enumerate(
            [(rows_in, rows_v), (lens_in, lens_s), (win, win_v), (wout, wout_v)]
        )
    ]
    for load in loads:
        load.start()
    tokens = hid_v.shape[0] // CHUNKS
    chunk_loads = []
    for i in range(CHUNKS):
        at = pl.ds(i * tokens, tokens)
        chunk_loads.append((
            pltpu.make_async_copy(hid.at[at], hid_v.at[at], hid_sem.at[i]),
            pltpu.make_async_copy(grad.at[at], grad_v.at[at], grad_sem.at[i]),
        ))
    for i, pair in enumerate(chunk_loads[:AHEAD]):
        for load in pair:
            load.start(priority=int(i > 0))

    x_peers = [(dp, lax.rem(x + d, NX) * 2 + zh) for d in (1, 2, 3)]
    z_peer = (dp, x * 2 + 1 - zh)
    y_peers = [(zl * 8 + lax.rem(y + d, NY) * 2 + core, tn) for d in (1, 2, 3)]
    core_peer = (zl * 8 + y * 2 + 1 - core, tn)
    q_y = (y % 2) * 2 + zh
    q_targets = [(z * 8 + q_y * 2 + 1 - core, zl * 2 + y // 2) for z in range(NZ)]
    q_sources = [(x * 8 + (zh * 2 + y // 2) * 2 + 1 - core, z * 2 + y % 2) for z in range(NX)]
    row_sources = [(z * 8 + x * 2 + core, zl * 2 + (zh + crossed(z, zl)) % 2) for z in range(NZ)]
    row_zh = (zh + crossed(zl, x)) % 2
    self_row = x == zl
    barrier = pltpu.get_barrier_semaphore()

    def signal(sem, devices):
        for device in devices:
            pl.semaphore_signal(sem, inc=1, device_id=device, device_id_type=MESH)

    own_source = (x == zl) & (x == y)
    signal(barrier, [*q_sources, z_peer, *x_peers, *y_peers, core_peer])
    for z, device in enumerate(row_sources):

        @pl.when(jnp.logical_not(own_source & (z == zl)))
        def _(device=device):
            signal(barrier, [device])

    sig_copy = pltpu.make_async_copy(sigma_v, sigma_s, sig_sem)
    loads[1].wait()
    for load in loads[2:]:
        load.wait()
    wide_in[...] = jnp.concatenate([win_v[...], jnp.zeros_like(win_v)], axis=0).T
    wide_out[...] = jnp.concatenate([jnp.zeros_like(wout_v), wout_v[...]], axis=0).T

    q_copies = []
    position = lax.broadcasted_iota(jnp.int32, (LEN, 2 * R), 0)
    for i in range(CHUNKS):
        at = pl.ds(i * tokens, tokens)
        for load in chunk_loads[i]:
            load.wait()
        if i + AHEAD < CHUNKS:
            for load in chunk_loads[i + AHEAD]:
                load.start(priority=1)
        out = jnp.dot(hid_v[at, :], wide_in[...], preferred_element_type=jnp.float32)
        out += jnp.dot(grad_v[at, :], wide_out[...], preferred_element_type=jnp.float32)
        for j in range(tokens // LEN):
            s = i * (tokens // LEN) + j
            block = jnp.where(position < lens_s[s], out[j * LEN : (j + 1) * LEN], 0.0)
            part[s] = block
            coded[s], scale[s : s + 1, :] = quantize(block)
        if i == 2:
            loads[0].wait()
            sigma_v[...] = jnp.broadcast_to(own_order(rows_v[...], dp), sigma_v.shape)
            sig_copy.start()
        if i == GREET:
            pl.semaphore_wait(barrier, 16 - own_source.astype(jnp.int32))
            signal(known_sem.at[0], y_peers)
            for z, device in enumerate(q_targets):
                q_copies.append(
                    remote(queries, qall.at[1 - core, q_y, x], qs_sem.at[z], qr_sem.at[x], device)
                )
                q_copies[-1].start()

    sig_copy.wait()

    def store_block(xx, k, h):
        return xx * 8 + lax.rem(2 * k + h + dp, 8)

    def source(xx, k, h):
        return sigma_s[store_block(xx, k, h), 0]

    x_copies, xc_copies = {}, []
    for d in (2, 1, 3):
        for k in range(STEPS):
            for h in range(2):
                s = source(lax.rem(x + d, NX), k, h)
                xsscale[d - 1, 2 * k + h : 2 * k + h + 1, :] = scale[pl.ds(s, 1), :]
        copy = remote(xsscale.at[d - 1], xrscale.at[d - 1], xcs_sem.at[d - 1], xcr_sem.at[d - 1], x_peers[d - 1])
        copy.start()
        xc_copies.append(copy)
    for k in range(STEPS):
        for d in (2, 1, 3):
            for h in range(2):
                xsend[d - 1, k, h] = coded[source(lax.rem(x + d, NX), k, h)]
            n = (d - 1) * STEPS + k
            copy = remote(xsend.at[d - 1, k], xrecv.at[d - 1, k], xs_sem.at[n], xr_sem.at[n], x_peers[d - 1])
            copy.start()
            x_copies[k, d] = copy

    for copy in xc_copies:
        copy.wait_recv()
    z_copies, zc_copies, b_copies = [], [], []

    def z_step(k):
        for d in (2, 1, 3):
            x_copies[k, d].wait_recv()
        for h in range(2):
            total = part[source(x, k, h)]
            for d in (1, 2, 3):
                n = 2 * k + h
                total += dequantize(xrecv[d - 1, k, h], xrscale[d - 1, n : n + 1, :])
            zsend[k, h], zsscale[k, h : h + 1, :] = quantize(total)
        z_copies.append(remote(zsend.at[k], zrecv.at[k], zs_sem.at[k], zr_sem.at[k], z_peer))
        z_copies[-1].start()
        zc_copies.append(remote(zsscale.at[k], zrscale.at[k], zcs_sem.at[k], zcr_sem.at[k], z_peer))
        zc_copies[-1].start()

    def b_step(k):
        z_copies[k].wait_recv()
        zc_copies[k].wait_recv()
        for h in range(2):
            total = dequantize(zsend[k, h], zsscale[k, h : h + 1, :])
            total += dequantize(zrecv[k, h], zrscale[k, h : h + 1, :])
            kron = lax.dot_general(
                total[:, :R], total[:, R:], (((0,), (0,)), ((), ())),
                precision=lax.Precision.HIGHEST, preferred_element_type=jnp.float32,
            )
            mean = jnp.sum(jnp.sum(kron * kron, axis=0, keepdims=True), axis=1, keepdims=True) * (1.0 / (R * R))
            normed = kron * (1.0 / jnp.sqrt(mean + 1e-06))
            bsend[2 * k + h] = normed.reshape(R * R // 128, 128).astype(jnp.bfloat16)
        for h in range(2):
            q = store_block(x, k, h)
            row = bsend.at[2 * k + h]
            for d in (2, 1, 3, 0):
                n = (2 * k + h) * NX + d
                copy = remote(row, brecv.at[dp], bs_sem.at[n], br_sem, (q, lax.rem(x + d, NX) * 2 + row_zh))
                if k == 0 and h == 0 and d == 0:

                    @pl.when(self_row)
                    def _(row=row):
                        pltpu.make_async_copy(row, brecv.at[dp], br_sem).start()

                    @pl.when(jnp.logical_not(self_row))
                    def _(copy=copy):
                        copy.start()

                    first_copy.append(copy)
                else:
                    copy.start()
                    b_copies.append(copy)

    first_copy = []
    z_step(0)
    mine = qall.at[core, y]
    for i in range(NX):
        pltpu.make_async_copy(queries, mine.at[i], qr_sem.at[i]).wait()
    for d, device in enumerate(y_peers):
        q_copies.append(remote(mine, mine, qs_sem.at[4 + d], qr_sem.at[4 + d], device))
        q_copies[-1].start()
    z_step(1)
    pl.semaphore_wait(known_sem.at[0], 3)
    signal(known_sem.at[1], [core_peer])
    z_step(2)
    z_step(3)
    pl.semaphore_wait(known_sem.at[1], 1)
    for k in range(STEPS):
        b_step(k)
    for copy in q_copies[4:]:
        copy.wait_recv()
    mine = qall.at[core]
    q_copies.append(remote(mine, mine, qs_sem.at[7], qr_sem.at[7], core_peer))
    q_copies[-1].start()

    holder, _, block, row = tables(rows_v[...])
    slot = pick(holder, row, block == dp)
    place = lax.broadcasted_iota(jnp.int32, (DP, SEQ), 1) == slot
    q_copies[-1].wait_recv()

    pltpu.make_async_copy(brecv, brecv, br_sem).wait()
    flat[...] = brecv[...].reshape(flat.shape).astype(jnp.float32)
    cols = R * R // 128
    for a in range(cols):
        wide[:, a * 128 : (a + 1) * 128] = flat[pl.ds(a, DP, stride=cols), :].astype(jnp.bfloat16)
    ordered = place.astype(jnp.bfloat16)
    mine = wide[:, pl.ds(pl.multiple_of(tn * QCOLS, QCOLS), QCOLS)]
    store_ref[...] = lax.dot_general(
        ordered, mine, (((0,), (0,)), ((), ())), preferred_element_type=jnp.float32
    ).astype(jnp.bfloat16)
    total = jnp.zeros((DP, 4 * QROWS), jnp.float32)
    for c in range(TP):
        block = jnp.concatenate(
            [qall[1 - m % 2, (m // 2) * 2 + c % 2, c // 2] for m in range(4)], axis=0
        )
        total += lax.dot_general(
            wide[:, c * QCOLS : (c + 1) * QCOLS], block, (((1,), (1,)), ((), ())), preferred_element_type=jnp.float32
        )
    scores_ref[...] = lax.dot_general(
        place.astype(jnp.float32), total, (((0,), (0,)), ((), ())),
        precision=lax.Precision.HIGHEST, preferred_element_type=jnp.float32,
    ) * (1.0 / R)

    for copy in [*q_copies, *xc_copies, *x_copies.values(), *z_copies, *zc_copies, *b_copies]:
        copy.wait_send()

    @pl.when(jnp.logical_not(self_row))
    def _():
        first_copy[0].wait_send()


def per_device(hidden_in, grad_out, proj_in, proj_out, lengths, store_row, queries):
    rows = store_row.reshape(-1, 128)
    dma, vmem = pltpu.SemaphoreType.DMA, pltpu.VMEM
    bf16, f32, i16, i32 = jnp.bfloat16, jnp.float32, jnp.int16, jnp.int32
    tokens, wide_k = hidden_in.shape
    narrow_k = grad_out.shape[1]
    return pl.pallas_call(
        kernel,
        out_shape=(
            jax.ShapeDtypeStruct((SEQ, QCOLS), bf16),
            jax.ShapeDtypeStruct((SEQ, 4 * QROWS), f32),
        ),
        in_specs=[pl.BlockSpec(memory_space=pltpu.HBM)] * 7,
        out_specs=(pl.BlockSpec(memory_space=pltpu.VMEM),) * 2,
        scratch_shapes=[
            vmem((tokens, wide_k), bf16), vmem((tokens, narrow_k), bf16),
            vmem((R, wide_k), bf16), vmem((R, narrow_k), bf16),
            vmem((wide_k, 2 * R), bf16), vmem((narrow_k, 2 * R), bf16),
            pltpu.SMEM((SEQ,), i32), vmem(rows.shape, i32),
            vmem((DP, 128), i32), pltpu.SMEM((DP, 128), i32),
            vmem((SEQ, LEN, 2 * R), f32), vmem((SEQ, LEN, 2 * R), i16), vmem((SEQ, 2 * R), f32),
            vmem((3, STEPS, 2, LEN, 2 * R), i16), vmem((3, 2 * STEPS, 2 * R), f32),
            vmem((3, STEPS, 2, LEN, 2 * R), i16), vmem((3, 2 * STEPS, 2 * R), f32),
            vmem((STEPS, 2, LEN, 2 * R), i16), vmem((STEPS, 2, 2 * R), f32),
            vmem((STEPS, 2, LEN, 2 * R), i16), vmem((STEPS, 2, 2 * R), f32),
            vmem((2 * STEPS, 32, 128), bf16), vmem((DP, 32, 128), bf16),
            vmem((2, NY, NX, QROWS, QCOLS), bf16), vmem((DP * 32, 128), f32), vmem((DP, R * R), bf16),
            dma((4,)), dma((CHUNKS,)), dma((CHUNKS,)), dma,
            dma((3 * STEPS,)), dma((3 * STEPS,)), dma((3,)), dma((3,)),
            dma((STEPS,)), dma((STEPS,)), dma((STEPS,)), dma((STEPS,)),
            dma((2 * STEPS * NX,)), dma, dma((8,)), dma((8,)), pltpu.SemaphoreType.REGULAR((2,)),
        ],
        compiler_params=pltpu.CompilerParams(collective_id=0, has_side_effects=True, vmem_limit_bytes=63 * 2**20),
    )(hidden_in, grad_out, proj_in.T, proj_out.T, lengths, rows, queries)


def solution(mesh):
    placed = (
        P("dp", "tensor"), P("dp", "tensor"), P("tensor", None), P("tensor", None),
        P("dp"), P(), P("dp", "tensor"),
    )
    return jax.shard_map(
        per_device, mesh=mesh, in_specs=placed, out_specs=(P("dp", "tensor"), P("dp", "tensor")), check_vma=False
    )
```

```python
import jax
import jax.numpy as jnp
from jax import lax
from jax.experimental import pallas as pl
from jax.experimental.pallas import tpu as pltpu
from jax.sharding import PartitionSpec as P

MESH = pl.DeviceIdType.MESH
DP, TP = 32, 8
NX, NY, NZ = 4, 4, 4
SEQ, LEN, R = 32, 64, 64
STEPS = 4
CHUNKS = 8
AHEAD = 4
FAR_FIRST = (2, 1, 3, 0)
GREET = 1
QROWS, QCOLS = 32, 512
TOP = 32767.0


def quantize(block):
    peak = jnp.maximum(jnp.max(jnp.abs(block), axis=0, keepdims=True), 1e-30)
    values = jnp.round(block * (TOP / peak)).astype(jnp.int32).astype(jnp.int16)
    return values, peak * (1.0 / TOP)


def dequantize(values, scale):
    return values.astype(jnp.int32).astype(jnp.float32) * scale


def crossed(a, b):
    return ((a - b == 3) | (b - a == 3)).astype(jnp.int32)


def tables(rows):
    at = lax.broadcasted_iota(jnp.int32, rows.shape, 0) * 128 + lax.broadcasted_iota(jnp.int32, rows.shape, 1)
    high, low = lambda v: lax.shift_right_logical(v, 5), lambda v: lax.bitwise_and(v, 31)
    return high(at), low(at), high(rows), low(rows)


def pick(keys, values, mask):
    keys = jnp.where(mask, keys, -1)
    each = lax.broadcasted_iota(jnp.int32, (DP, *keys.shape), 0)
    found = jnp.sum(jnp.where(keys[None] == each, values[None], 0), axis=1)
    return jnp.sum(found, axis=1, keepdims=True)


def own_order(rows, dp):
    holder, number, block, _ = tables(rows)
    return jnp.minimum(pick(block, number, holder == dp), SEQ - 1)


def kernel(
    hid, grad, win, wout, lens_in, rows_in, queries, store_ref, scores_ref,
    hid_v, grad_v, win_v, wout_v, wide_in, wide_out, lens_s, rows_v, sigma_v, sigma_s,
    part, coded, scale, xsend, xsscale, xrecv, xrscale, zsend, zsscale, zrecv, zrscale,
    bsend, brecv, qall, flat, wide,
    load_sem, hid_sem, grad_sem, sig_sem, xs_sem, xr_sem, xcs_sem, xcr_sem,
    zs_sem, zr_sem, zcs_sem, zcr_sem, bs_sem, br_sem, qs_sem, qr_sem, known_sem,
):
    dp, tn = lax.axis_index("dp"), lax.axis_index("tensor")
    zl, y, core = dp // 8, (dp // 2) % 4, dp % 2
    x, zh = tn // 2, tn % 2

    def remote(src, dst, send, recv, device):
        return pltpu.make_async_remote_copy(
            src_ref=src, dst_ref=dst, send_sem=send, recv_sem=recv, device_id=device, device_id_type=MESH
        )

    loads = [
        pltpu.make_async_copy(src, dst, load_sem.at[i])
        for i, (src, dst) in enumerate(
            [(rows_in, rows_v), (lens_in, lens_s), (win, win_v), (wout, wout_v)]
        )
    ]
    for load in loads:
        load.start()
    tokens = hid_v.shape[0] // CHUNKS
    chunk_loads = []
    for i in range(CHUNKS):
        at = pl.ds(i * tokens, tokens)
        chunk_loads.append((
            pltpu.make_async_copy(hid.at[at], hid_v.at[at], hid_sem.at[i]),
            pltpu.make_async_copy(grad.at[at], grad_v.at[at], grad_sem.at[i]),
        ))
    for i, pair in enumerate(chunk_loads[:AHEAD]):
        for load in pair:
            load.start(priority=int(i > 0))

    x_peers = [(dp, lax.rem(x + d, NX) * 2 + zh) for d in (1, 2, 3)]
    z_peer = (dp, x * 2 + 1 - zh)
    y_peers = [(zl * 8 + lax.rem(y + d, NY) * 2 + core, tn) for d in (1, 2, 3)]
    core_peer = (zl * 8 + y * 2 + 1 - core, tn)
    q_y = (y % 2) * 2 + zh
    q_targets = [(z * 8 + q_y * 2 + 1 - core, zl * 2 + y // 2) for z in range(NZ)]
    q_sources = [(x * 8 + (zh * 2 + y // 2) * 2 + 1 - core, z * 2 + y % 2) for z in range(NX)]
    row_sources = [
        (z * 8 + lax.rem(x - y - zl - z + 3 * NY, NY) * 2 + core, x * 2 + (zh + crossed(z, zl)) % 2) for z in range(NZ)
    ]
    row_peers = [
        (zl * 8 + lax.rem(y + d, NY) * 2 + core, lax.rem(x + d, NX) * 2 + zh) for d in (1, 2, 3)
    ]
    self_row = x == 2 * ((zl + y) % 2)
    barrier = pltpu.get_barrier_semaphore()

    def signal(sem, devices):
        for device in devices:
            pl.semaphore_signal(sem, inc=1, device_id=device, device_id_type=MESH)

    signal(barrier, [*q_sources, z_peer, *x_peers, *y_peers, core_peer, *row_peers])
    for z, device in enumerate(row_sources):

        @pl.when(jnp.logical_not(self_row & (z == zl)))
        def _(device=device):
            signal(barrier, [device])

    sig_copy = pltpu.make_async_copy(sigma_v, sigma_s, sig_sem)
    loads[1].wait()
    for load in loads[2:]:
        load.wait()
    wide_in[...] = jnp.concatenate([win_v[...], jnp.zeros_like(win_v)], axis=0).T
    wide_out[...] = jnp.concatenate([jnp.zeros_like(wout_v), wout_v[...]], axis=0).T

    q_copies = []
    position = lax.broadcasted_iota(jnp.int32, (LEN, 2 * R), 0)
    for i in range(CHUNKS):
        at = pl.ds(i * tokens, tokens)
        for load in chunk_loads[i]:
            load.wait()
        if i + AHEAD < CHUNKS:
            for load in chunk_loads[i + AHEAD]:
                load.start(priority=1)
        out = jnp.dot(hid_v[at, :], wide_in[...], preferred_element_type=jnp.float32)
        out += jnp.dot(grad_v[at, :], wide_out[...], preferred_element_type=jnp.float32)
        for j in range(tokens // LEN):
            s = i * (tokens // LEN) + j
            block = jnp.where(position < lens_s[s], out[j * LEN : (j + 1) * LEN], 0.0)
            part[s] = block
            coded[s], scale[s : s + 1, :] = quantize(block)
        if i == 2:
            loads[0].wait()
            sigma_v[...] = jnp.broadcast_to(own_order(rows_v[...], dp), sigma_v.shape)
            sig_copy.start()
        if i == GREET:
            pl.semaphore_wait(barrier, 19 - self_row.astype(jnp.int32))
            signal(known_sem.at[0], row_peers)
            for z, device in enumerate(q_targets):
                q_copies.append(
                    remote(queries, qall.at[1 - core, q_y, x], qs_sem.at[z], qr_sem.at[x], device)
                )
                q_copies[-1].start()

    sig_copy.wait()

    def store_z(k):
        return lax.rem(zl + FAR_FIRST[k], NZ)

    def store_block(xx, k, h):
        z = store_z(k)
        return z * 8 + lax.rem(xx - y - zl - z + 3 * NY, NY) * 2 + (core + h) % 2

    def source(xx, k, h):
        return sigma_s[store_block(xx, k, h), 0]

    x_copies, xc_copies = {}, []
    for d in (2, 1, 3):
        for k in range(STEPS):
            for h in range(2):
                s = source(lax.rem(x + d, NX), k, h)
                xsscale[d - 1, 2 * k + h : 2 * k + h + 1, :] = scale[pl.ds(s, 1), :]
        copy = remote(xsscale.at[d - 1], xrscale.at[d - 1], xcs_sem.at[d - 1], xcr_sem.at[d - 1], x_peers[d - 1])
        copy.start()
        xc_copies.append(copy)
    for k in range(STEPS):
        for d in (2, 1, 3):
            for h in range(2):
                xsend[d - 1, k, h] = coded[source(lax.rem(x + d, NX), k, h)]
            n = (d - 1) * STEPS + k
            copy = remote(xsend.at[d - 1, k], xrecv.at[d - 1, k], xs_sem.at[n], xr_sem.at[n], x_peers[d - 1])
            copy.start()
            x_copies[k, d] = copy

    for copy in xc_copies:
        copy.wait_recv()
    z_copies, zc_copies, b_copies = [], [], []

    def z_step(k):
        for d in (2, 1, 3):
            x_copies[k, d].wait_recv()
        for h in range(2):
            total = part[source(x, k, h)]
            for d in (1, 2, 3):
                n = 2 * k + h
                total += dequantize(xrecv[d - 1, k, h], xrscale[d - 1, n : n + 1, :])
            zsend[k, h], zsscale[k, h : h + 1, :] = quantize(total)
        z_copies.append(remote(zsend.at[k], zrecv.at[k], zs_sem.at[k], zr_sem.at[k], z_peer))
        z_copies[-1].start()
        zc_copies.append(remote(zsscale.at[k], zrscale.at[k], zcs_sem.at[k], zcr_sem.at[k], z_peer))
        zc_copies[-1].start()

    def b_step(k):
        z_copies[k].wait_recv()
        zc_copies[k].wait_recv()
        for h in range(2):
            total = dequantize(zsend[k, h], zsscale[k, h : h + 1, :])
            total += dequantize(zrecv[k, h], zrscale[k, h : h + 1, :])
            kron = lax.dot_general(
                total[:, :R], total[:, R:], (((0,), (0,)), ((), ())),
                precision=lax.Precision.HIGHEST, preferred_element_type=jnp.float32,
            )
            mean = jnp.sum(jnp.sum(kron * kron, axis=0, keepdims=True), axis=1, keepdims=True) * (1.0 / (R * R))
            normed = kron * (1.0 / jnp.sqrt(mean + 1e-06))
            bsend[2 * k + h] = normed.reshape(R * R // 128, 128).astype(jnp.bfloat16)
        for h in range(2):
            q, near = store_block(x, k, h), (zh + crossed(zl, store_z(k))) % 2
            row = bsend.at[2 * k + h]
            for d in (2, 1, 3, 0):
                n = (2 * k + h) * NX + d
                copy = remote(row, brecv.at[dp], bs_sem.at[n], br_sem, (q, lax.rem(x + d, NX) * 2 + near))
                if FAR_FIRST[k] == 0 and h == 0 and d == 0:

                    @pl.when(self_row)
                    def _(row=row):
                        pltpu.make_async_copy(row, brecv.at[dp], br_sem).start()

                    @pl.when(jnp.logical_not(self_row))
                    def _(copy=copy):
                        copy.start()

                    first_copy.append(copy)
                else:
                    copy.start()
                    b_copies.append(copy)

    first_copy = []
    z_step(0)
    mine = qall.at[core, y]
    for i in range(NX):
        pltpu.make_async_copy(queries, mine.at[i], qr_sem.at[i]).wait()
    for d, device in enumerate(y_peers):
        q_copies.append(remote(mine, mine, qs_sem.at[4 + d], qr_sem.at[4 + d], device))
        q_copies[-1].start()
    z_step(1)
    pl.semaphore_wait(known_sem.at[0], 3)
    signal(known_sem.at[1], [core_peer])
    z_step(2)
    z_step(3)
    pl.semaphore_wait(known_sem.at[1], 1)
    for k in range(STEPS):
        b_step(k)
    for copy in q_copies[4:]:
        copy.wait_recv()
    mine = qall.at[core]
    q_copies.append(remote(mine, mine, qs_sem.at[7], qr_sem.at[7], core_peer))
    q_copies[-1].start()

    holder, _, block, row = tables(rows_v[...])
    slot = pick(holder, row, block == dp)
    place = lax.broadcasted_iota(jnp.int32, (DP, SEQ), 1) == slot
    q_copies[-1].wait_recv()

    pltpu.make_async_copy(brecv, brecv, br_sem).wait()
    flat[...] = brecv[...].reshape(flat.shape).astype(jnp.float32)
    cols = R * R // 128
    for a in range(cols):
        wide[:, a * 128 : (a + 1) * 128] = flat[pl.ds(a, DP, stride=cols), :].astype(jnp.bfloat16)
    ordered = place.astype(jnp.bfloat16)
    mine = wide[:, pl.ds(pl.multiple_of(tn * QCOLS, QCOLS), QCOLS)]
    store_ref[...] = lax.dot_general(
        ordered, mine, (((0,), (0,)), ((), ())), preferred_element_type=jnp.float32
    ).astype(jnp.bfloat16)
    total = jnp.zeros((DP, 4 * QROWS), jnp.float32)
    for c in range(TP):
        block = jnp.concatenate(
            [qall[1 - m % 2, (m // 2) * 2 + c % 2, c // 2] for m in range(4)], axis=0
        )
        total += lax.dot_general(
            wide[:, c * QCOLS : (c + 1) * QCOLS], block, (((1,), (1,)), ((), ())), preferred_element_type=jnp.float32
        )
    scores_ref[...] = lax.dot_general(
        place.astype(jnp.float32), total, (((0,), (0,)), ((), ())),
        precision=lax.Precision.HIGHEST, preferred_element_type=jnp.float32,
    ) * (1.0 / R)

    for copy in [*q_copies, *xc_copies, *x_copies.values(), *z_copies, *zc_copies, *b_copies]:
        copy.wait_send()

    @pl.when(jnp.logical_not(self_row))
    def _():
        first_copy[0].wait_send()


def per_device(hidden_in, grad_out, proj_in, proj_out, lengths, store_row, queries):
    rows = store_row.reshape(-1, 128)
    dma, vmem = pltpu.SemaphoreType.DMA, pltpu.VMEM
    bf16, f32, i16, i32 = jnp.bfloat16, jnp.float32, jnp.int16, jnp.int32
    tokens, wide_k = hidden_in.shape
    narrow_k = grad_out.shape[1]
    return pl.pallas_call(
        kernel,
        out_shape=(
            jax.ShapeDtypeStruct((SEQ, QCOLS), bf16),
            jax.ShapeDtypeStruct((SEQ, 4 * QROWS), f32),
        ),
        in_specs=[pl.BlockSpec(memory_space=pltpu.HBM)] * 7,
        out_specs=(pl.BlockSpec(memory_space=pltpu.VMEM),) * 2,
        scratch_shapes=[
            vmem((tokens, wide_k), bf16), vmem((tokens, narrow_k), bf16),
            vmem((R, wide_k), bf16), vmem((R, narrow_k), bf16),
            vmem((wide_k, 2 * R), bf16), vmem((narrow_k, 2 * R), bf16),
            pltpu.SMEM((SEQ,), i32), vmem(rows.shape, i32),
            vmem((DP, 128), i32), pltpu.SMEM((DP, 128), i32),
            vmem((SEQ, LEN, 2 * R), f32), vmem((SEQ, LEN, 2 * R), i16), vmem((SEQ, 2 * R), f32),
            vmem((3, STEPS, 2, LEN, 2 * R), i16), vmem((3, 2 * STEPS, 2 * R), f32),
            vmem((3, STEPS, 2, LEN, 2 * R), i16), vmem((3, 2 * STEPS, 2 * R), f32),
            vmem((STEPS, 2, LEN, 2 * R), i16), vmem((STEPS, 2, 2 * R), f32),
            vmem((STEPS, 2, LEN, 2 * R), i16), vmem((STEPS, 2, 2 * R), f32),
            vmem((2 * STEPS, 32, 128), bf16), vmem((DP, 32, 128), bf16),
            vmem((2, NY, NX, QROWS, QCOLS), bf16), vmem((DP * 32, 128), f32), vmem((DP, R * R), bf16),
            dma((4,)), dma((CHUNKS,)), dma((CHUNKS,)), dma,
            dma((3 * STEPS,)), dma((3 * STEPS,)), dma((3,)), dma((3,)),
            dma((STEPS,)), dma((STEPS,)), dma((STEPS,)), dma((STEPS,)),
            dma((2 * STEPS * NX,)), dma, dma((8,)), dma((8,)), pltpu.SemaphoreType.REGULAR((2,)),
        ],
        compiler_params=pltpu.CompilerParams(collective_id=0, has_side_effects=True, vmem_limit_bytes=63 * 2**20),
    )(hidden_in, grad_out, proj_in.T, proj_out.T, lengths, rows, queries)


def solution(mesh):
    placed = (
        P("dp", "tensor"), P("dp", "tensor"), P("tensor", None), P("tensor", None),
        P("dp"), P(), P("dp", "tensor"),
    )
    return jax.shard_map(
        per_device, mesh=mesh, in_specs=placed, out_specs=(P("dp", "tensor"), P("dp", "tensor")), check_vma=False
    )
```

```python
import jax
import jax.numpy as jnp
from jax import lax
from jax.experimental import pallas as pl
from jax.experimental.pallas import tpu as pltpu
from jax.sharding import PartitionSpec as P

MESH = pl.DeviceIdType.MESH
DP, TP = 32, 8
NX, NY, NZ = 4, 4, 4
SEQ, LEN, R = 32, 64, 64
STEPS = 4
CHUNKS = 8
FAR_FIRST = (2, 1, 3, 0)
GREET, CUTS = (0, 3, 7), (6, 4)
QROWS, QCOLS = 32, 512
TOP = 32767.0


def quantize(block):
    peak = jnp.maximum(jnp.max(jnp.abs(block), axis=0, keepdims=True), 1e-30)
    values = jnp.round(block * (TOP / peak)).astype(jnp.int32).astype(jnp.int16)
    return values, peak * (1.0 / TOP)


def dequantize(values, scale):
    return values.astype(jnp.int32).astype(jnp.float32) * scale


def crossed(a, b):
    return ((a - b == 3) | (b - a == 3)).astype(jnp.int32)


def tables(rows):
    at = lax.broadcasted_iota(jnp.int32, rows.shape, 0) * 128 + lax.broadcasted_iota(jnp.int32, rows.shape, 1)
    high, low = lambda v: lax.shift_right_logical(v, 5), lambda v: lax.bitwise_and(v, 31)
    return high(at), low(at), high(rows), low(rows)


def pick(keys, values, mask):
    keys = jnp.where(mask, keys, -1)
    each = lax.broadcasted_iota(jnp.int32, (DP, *keys.shape), 0)
    found = jnp.sum(jnp.where(keys[None] == each, values[None], 0), axis=1)
    return jnp.sum(found, axis=1, keepdims=True)


def own_order(rows, dp):
    holder, number, block, _ = tables(rows)
    return jnp.minimum(pick(block, number, holder == dp), SEQ - 1)


def kernel(
    hid, grad, win, wout, lens_in, rows_in, queries, store_ref, scores_ref,
    hid_v, grad_v, win_v, wout_v, wide_in, wide_out, lens_s, rows_v, sigma_v, sigma_s,
    part, coded, scale, xsend, xsscale, xrecv, xrscale, zsend, zsscale, zrecv, zrscale,
    bsend, brecv, qall, flat, wide,
    load_sem, hid_sem, grad_sem, sig_sem, xs_sem, xr_sem, xcs_sem, xcr_sem,
    zs_sem, zr_sem, zcs_sem, zcr_sem, bs_sem, br_sem, qs_sem, qr_sem, known_sem,
):
    dp, tn = lax.axis_index("dp"), lax.axis_index("tensor")
    zl, y, core = dp // 8, (dp // 2) % 4, dp % 2
    x, zh = tn // 2, tn % 2

    def remote(src, dst, send, recv, device):
        return pltpu.make_async_remote_copy(
            src_ref=src, dst_ref=dst, send_sem=send, recv_sem=recv, device_id=device, device_id_type=MESH
        )

    loads = [
        pltpu.make_async_copy(src, dst, load_sem.at[i])
        for i, (src, dst) in enumerate(
            [(rows_in, rows_v), (lens_in, lens_s), (win, win_v), (wout, wout_v)]
        )
    ]
    for load in loads:
        load.start()
    tokens = hid_v.shape[0] // CHUNKS
    chunk_loads = []
    for i in range(CHUNKS):
        at = pl.ds(i * tokens, tokens)
        chunk_loads.append((
            pltpu.make_async_copy(hid.at[at], hid_v.at[at], hid_sem.at[i]),
            pltpu.make_async_copy(grad.at[at], grad_v.at[at], grad_sem.at[i]),
        ))
    def load_chunks(first, last):
        for pair in chunk_loads[first:last]:
            for load in pair:
                load.start(priority=int(first > 0))

    load_chunks(0, 1)
    load_chunks(1, 4)

    x_peers = [(dp, lax.rem(x + d, NX) * 2 + zh) for d in (1, 2, 3)]
    z_peer = (dp, x * 2 + 1 - zh)
    y_peers = [(zl * 8 + lax.rem(y + d, NY) * 2 + core, tn) for d in (1, 2, 3)]
    core_peer = (zl * 8 + y * 2 + 1 - core, tn)
    q_y = (y % 2) * 2 + zh
    q_targets = [(z * 8 + q_y * 2 + 1 - core, zl * 2 + y // 2) for z in range(NZ)]
    q_sources = [(x * 8 + (zh * 2 + y // 2) * 2 + 1 - core, z * 2 + y % 2) for z in range(NX)]
    row_sources = [
        (z * 8 + lax.rem(x - y - zl - z + 3 * NY, NY) * 2 + core, x * 2 + (zh + crossed(z, zl)) % 2) for z in range(NZ)
    ]
    row_peers = [
        (zl * 8 + lax.rem(y + d, NY) * 2 + core, lax.rem(x + d, NX) * 2 + zh) for d in (1, 2, 3)
    ]
    self_row = x == 2 * ((zl + y) % 2)
    barrier = pltpu.get_barrier_semaphore()

    def signal(sem, devices):
        for device in devices:
            pl.semaphore_signal(sem, inc=1, device_id=device, device_id_type=MESH)

    signal(barrier, [z_peer, *q_sources])
    for z, device in enumerate(row_sources):

        @pl.when(jnp.logical_not(self_row & (z == zl)))
        def _(device=device):
            signal(barrier, [device])

    load_chunks(4, 6)
    signal(barrier, [*x_peers, *y_peers, core_peer, *row_peers])
    load_chunks(6, CHUNKS)
    sig_copy = pltpu.make_async_copy(sigma_v, sigma_s, sig_sem)
    loads[1].wait()
    for load in loads[2:]:
        load.wait()
    wide_in[...] = jnp.concatenate([win_v[...], jnp.zeros_like(win_v)], axis=0).T
    wide_out[...] = jnp.concatenate([jnp.zeros_like(wout_v), wout_v[...]], axis=0).T

    q_copies = [
        remote(queries, qall.at[1 - core, q_y, x], qs_sem.at[z], qr_sem.at[x], device)
        for z, device in enumerate(q_targets)
    ]
    def ring(at, size):
        return jnp.minimum(at, size - at)

    hops = ring(x, NX) + ring(y, NY) + ring(zh * NZ + zl, 2 * NZ)
    turns = [hops >= CUTS[0], (hops < CUTS[0]) & (hops >= CUTS[1]), hops < CUTS[1]]
    position = lax.broadcasted_iota(jnp.int32, (LEN, 2 * R), 0)
    for i in range(CHUNKS):
        at = pl.ds(i * tokens, tokens)
        for load in chunk_loads[i]:
            load.wait()
        out = jnp.dot(hid_v[at, :], wide_in[...], preferred_element_type=jnp.float32)
        out += jnp.dot(grad_v[at, :], wide_out[...], preferred_element_type=jnp.float32)
        for j in range(tokens // LEN):
            s = i * (tokens // LEN) + j
            block = jnp.where(position < lens_s[s], out[j * LEN : (j + 1) * LEN], 0.0)
            part[s] = block
            coded[s], scale[s : s + 1, :] = quantize(block)
        if i == 2:
            loads[0].wait()
            sigma_v[...] = jnp.broadcast_to(own_order(rows_v[...], dp), sigma_v.shape)
            sig_copy.start()
        for turn, here in enumerate(turns):
            if i == GREET[turn]:

                @pl.when(here)
                def _():
                    pl.semaphore_wait(barrier, 19 - self_row.astype(jnp.int32))
                    signal(known_sem.at[0], row_peers)
                    for copy in q_copies:
                        copy.start()

    sig_copy.wait()

    def store_z(k):
        return lax.rem(zl + FAR_FIRST[k], NZ)

    def store_block(xx, k, h):
        z = store_z(k)
        return z * 8 + lax.rem(xx - y - zl - z + 3 * NY, NY) * 2 + (core + h) % 2

    def source(xx, k, h):
        return sigma_s[store_block(xx, k, h), 0]

    x_copies, xc_copies = {}, []
    for k in range(STEPS):
        for d in (2, 1, 3):
            for h in range(2):
                xsend[d - 1, k, h] = coded[source(lax.rem(x + d, NX), k, h)]
            n = (d - 1) * STEPS + k
            copy = remote(xsend.at[d - 1, k], xrecv.at[d - 1, k], xs_sem.at[n], xr_sem.at[n], x_peers[d - 1])
            copy.start()
            x_copies[k, d] = copy
        for d in (2, 1, 3) if k == 0 else ():
            for kk in range(STEPS):
                for h in range(2):
                    s = source(lax.rem(x + d, NX), kk, h)
                    xsscale[d - 1, 2 * kk + h : 2 * kk + h + 1, :] = scale[pl.ds(s, 1), :]
            copy = remote(
                xsscale.at[d - 1], xrscale.at[d - 1], xcs_sem.at[d - 1], xcr_sem.at[d - 1], x_peers[d - 1]
            )
            copy.start()
            xc_copies.append(copy)

    for copy in xc_copies:
        copy.wait_recv()
    z_copies, zc_copies, b_copies = [], [], []

    def z_step(k):
        for d in (2, 1, 3):
            x_copies[k, d].wait_recv()
        for h in range(2):
            total = part[source(x, k, h)]
            for d in (1, 2, 3):
                n = 2 * k + h
                total += dequantize(xrecv[d - 1, k, h], xrscale[d - 1, n : n + 1, :])
            zsend[k, h], zsscale[k, h : h + 1, :] = quantize(total)
        z_copies.append(remote(zsend.at[k], zrecv.at[k], zs_sem.at[k], zr_sem.at[k], z_peer))
        z_copies[-1].start()
        zc_copies.append(remote(zsscale.at[k], zrscale.at[k], zcs_sem.at[k], zcr_sem.at[k], z_peer))
        zc_copies[-1].start()

    def b_step(k):
        z_copies[k].wait_recv()
        zc_copies[k].wait_recv()
        for h in range(2):
            total = dequantize(zsend[k, h], zsscale[k, h : h + 1, :])
            total += dequantize(zrecv[k, h], zrscale[k, h : h + 1, :])
            kron = lax.dot_general(
                total[:, :R], total[:, R:], (((0,), (0,)), ((), ())),
                precision=lax.Precision.HIGHEST, preferred_element_type=jnp.float32,
            )
            mean = jnp.sum(jnp.sum(kron * kron, axis=0, keepdims=True), axis=1, keepdims=True) * (1.0 / (R * R))
            normed = kron * (1.0 / jnp.sqrt(mean + 1e-06))
            bsend[2 * k + h] = normed.reshape(R * R // 128, 128).astype(jnp.bfloat16)
        for h in range(2):
            q, near = store_block(x, k, h), (zh + crossed(zl, store_z(k))) % 2
            row = bsend.at[2 * k + h]
            for d in (2, 1, 3, 0):
                n = (2 * k + h) * NX + d
                copy = remote(row, brecv.at[dp], bs_sem.at[n], br_sem, (q, lax.rem(x + d, NX) * 2 + near))
                if FAR_FIRST[k] == 0 and h == 0 and d == 0:

                    @pl.when(self_row)
                    def _(row=row):
                        pltpu.make_async_copy(row, brecv.at[dp], br_sem).start()

                    @pl.when(jnp.logical_not(self_row))
                    def _(copy=copy):
                        copy.start()

                    first_copy.append(copy)
                else:
                    copy.start()
                    b_copies.append(copy)

    first_copy = []
    z_step(0)
    z_step(1)
    mine = qall.at[core, y]
    for i in range(NX):
        pltpu.make_async_copy(queries, mine.at[i], qr_sem.at[i]).wait()
    for d, device in enumerate(y_peers):
        q_copies.append(remote(mine, mine, qs_sem.at[4 + d], qr_sem.at[4 + d], device))
        q_copies[-1].start()

    def to_core(d):
        block = qall.at[core, lax.rem(y + d, NY)]
        q_copies.append(remote(block, block, qs_sem.at[7 + d], qr_sem.at[7 + d], core_peer))
        q_copies[-1].start()

    to_core(0)
    pl.semaphore_wait(known_sem.at[0], 3)
    signal(known_sem.at[1], [core_peer])
    z_step(2)
    z_step(3)
    pl.semaphore_wait(known_sem.at[1], 1)
    for k in range(STEPS):
        b_step(k)
    for d in (1, 3, 2):
        block = qall.at[core, lax.rem(y + d, NY)]
        remote(block, block, qs_sem.at[3 + d], qr_sem.at[7 - d], core_peer).wait_recv()
        to_core(d)

    holder, _, block, row = tables(rows_v[...])
    slot = pick(holder, row, block == dp)
    place = lax.broadcasted_iota(jnp.int32, (DP, SEQ), 1) == slot
    for copy in q_copies[-4:]:
        copy.wait_recv()

    for copy in [*q_copies, *xc_copies, *x_copies.values(), *z_copies, *zc_copies, *b_copies]:
        copy.wait_send()

    @pl.when(jnp.logical_not(self_row))
    def _():
        first_copy[0].wait_send()

    pltpu.make_async_copy(brecv, brecv, br_sem).wait()
    flat[...] = brecv[...].reshape(flat.shape).astype(jnp.float32)
    cols = R * R // 128
    for a in range(cols):
        wide[:, a * 128 : (a + 1) * 128] = flat[pl.ds(a, DP, stride=cols), :].astype(jnp.bfloat16)
    ordered = place.astype(jnp.bfloat16)
    mine = wide[:, pl.ds(pl.multiple_of(tn * QCOLS, QCOLS), QCOLS)]
    store_ref[...] = lax.dot_general(
        ordered, mine, (((0,), (0,)), ((), ())), preferred_element_type=jnp.float32
    ).astype(jnp.bfloat16)
    total = jnp.zeros((DP, 4 * QROWS), jnp.float32)
    for c in range(TP):
        block = jnp.concatenate(
            [qall[1 - m % 2, (m // 2) * 2 + c % 2, c // 2] for m in range(4)], axis=0
        )
        total += lax.dot_general(
            wide[:, c * QCOLS : (c + 1) * QCOLS], block, (((1,), (1,)), ((), ())), preferred_element_type=jnp.float32
        )
    scores_ref[...] = lax.dot_general(
        place.astype(jnp.float32), total, (((0,), (0,)), ((), ())),
        precision=lax.Precision.HIGHEST, preferred_element_type=jnp.float32,
    ) * (1.0 / R)


def hand_over(store_in, scores_in, store_ref, scores_ref):
    store_ref[...] = store_in[...]
    scores_ref[...] = scores_in[...]


def per_device(hidden_in, grad_out, proj_in, proj_out, lengths, store_row, queries):
    rows = store_row.reshape(-1, 128)
    dma, vmem = pltpu.SemaphoreType.DMA, pltpu.VMEM
    bf16, f32, i16, i32 = jnp.bfloat16, jnp.float32, jnp.int16, jnp.int32
    tokens, wide_k = hidden_in.shape
    narrow_k = grad_out.shape[1]
    results = pl.pallas_call(
        kernel,
        out_shape=(
            jax.ShapeDtypeStruct((SEQ, QCOLS), bf16),
            jax.ShapeDtypeStruct((SEQ, 4 * QROWS), f32),
        ),
        in_specs=[pl.BlockSpec(memory_space=pltpu.HBM)] * 7,
        out_specs=(pl.BlockSpec(memory_space=pltpu.VMEM),) * 2,
        scratch_shapes=[
            vmem((tokens, wide_k), bf16), vmem((tokens, narrow_k), bf16),
            vmem((R, wide_k), bf16), vmem((R, narrow_k), bf16),
            vmem((wide_k, 2 * R), bf16), vmem((narrow_k, 2 * R), bf16),
            pltpu.SMEM((SEQ,), i32), vmem(rows.shape, i32),
            vmem((DP, 128), i32), pltpu.SMEM((DP, 128), i32),
            vmem((SEQ, LEN, 2 * R), f32), vmem((SEQ, LEN, 2 * R), i16), vmem((SEQ, 2 * R), f32),
            vmem((3, STEPS, 2, LEN, 2 * R), i16), vmem((3, 2 * STEPS, 2 * R), f32),
            vmem((3, STEPS, 2, LEN, 2 * R), i16), vmem((3, 2 * STEPS, 2 * R), f32),
            vmem((STEPS, 2, LEN, 2 * R), i16), vmem((STEPS, 2, 2 * R), f32),
            vmem((STEPS, 2, LEN, 2 * R), i16), vmem((STEPS, 2, 2 * R), f32),
            vmem((2 * STEPS, 32, 128), bf16), vmem((DP, 32, 128), bf16),
            vmem((2, NY, NX, QROWS, QCOLS), bf16), vmem((DP * 32, 128), f32), vmem((DP, R * R), bf16),
            dma((4,)), dma((CHUNKS,)), dma((CHUNKS,)), dma,
            dma((3 * STEPS,)), dma((3 * STEPS,)), dma((3,)), dma((3,)),
            dma((STEPS,)), dma((STEPS,)), dma((STEPS,)), dma((STEPS,)),
            dma((2 * STEPS * NX,)), dma, dma((11,)), dma((11,)), pltpu.SemaphoreType.REGULAR((2,)),
        ],
        compiler_params=pltpu.CompilerParams(collective_id=0, has_side_effects=True, vmem_limit_bytes=63 * 2**20),
    )(hidden_in, grad_out, proj_in.T, proj_out.T, lengths, rows, queries)
    whole = pl.BlockSpec(memory_space=vmem)
    return pl.pallas_call(
        hand_over,
        out_shape=tuple(jax.ShapeDtypeStruct(r.shape, r.dtype) for r in results),
        in_specs=[whole] * 2,
        out_specs=(whole,) * 2,
    )(*results)


def solution(mesh):
    placed = (
        P("dp", "tensor"), P("dp", "tensor"), P("tensor", None), P("tensor", None),
        P("dp"), P(), P("dp", "tensor"),
    )
    return jax.shard_map(
        per_device, mesh=mesh, in_specs=placed, out_specs=(P("dp", "tensor"), P("dp", "tensor")), check_vma=False
    )
```

```python
import jax
import jax.numpy as jnp
from jax import lax
from jax.experimental import pallas as pl
from jax.experimental.pallas import tpu as pltpu
from jax.sharding import PartitionSpec as P

MESH = pl.DeviceIdType.MESH
DP, TP = 32, 8
NX, NY, NZ = 4, 4, 4
SEQ, LEN, R = 32, 64, 64
STEPS = 4
CHUNKS = 8
FAR_FIRST = (2, 1, 3, 0)
GREET, CUTS = (0, 3, 7), (6, 4)
QROWS, QCOLS = 32, 512
TOP = 32767.0


def quantize(block):
    peak = jnp.maximum(jnp.max(jnp.abs(block), axis=0, keepdims=True), 1e-30)
    values = jnp.round(block * (TOP / peak)).astype(jnp.int32).astype(jnp.int16)
    return values, peak * (1.0 / TOP)


def dequantize(values, scale):
    return values.astype(jnp.int32).astype(jnp.float32) * scale


def crossed(a, b):
    return ((a - b == 3) | (b - a == 3)).astype(jnp.int32)


def tables(rows):
    at = lax.broadcasted_iota(jnp.int32, rows.shape, 0) * 128 + lax.broadcasted_iota(jnp.int32, rows.shape, 1)
    high, low = lambda v: lax.shift_right_logical(v, 5), lambda v: lax.bitwise_and(v, 31)
    return high(at), low(at), high(rows), low(rows)


def pick(keys, values, mask):
    keys = jnp.where(mask, keys, -1)
    each = lax.broadcasted_iota(jnp.int32, (DP, *keys.shape), 0)
    found = jnp.sum(jnp.where(keys[None] == each, values[None], 0), axis=1)
    return jnp.sum(found, axis=1, keepdims=True)


def own_order(rows, dp):
    holder, number, block, _ = tables(rows)
    return jnp.minimum(pick(block, number, holder == dp), SEQ - 1)


def kernel(
    hid, grad, win, wout, lens_in, rows_in, queries, store_ref, scores_ref,
    hid_v, grad_v, win_v, wout_v, wide_in, wide_out, lens_s, rows_v, sigma_v, sigma_s,
    part, coded, scale, xsend, xsscale, xrecv, xrscale, zsend, zsscale, zrecv, zrscale,
    bsend, brecv, qall, flat, wide,
    load_sem, hid_sem, grad_sem, sig_sem, xs_sem, xr_sem, xcs_sem, xcr_sem,
    zs_sem, zr_sem, zcs_sem, zcr_sem, bs_sem, br_sem, qs_sem, qr_sem, known_sem,
):
    dp, tn = lax.axis_index("dp"), lax.axis_index("tensor")
    zl, y, core = dp // 8, (dp // 2) % 4, dp % 2
    x, zh = tn // 2, tn % 2

    def remote(src, dst, send, recv, device):
        return pltpu.make_async_remote_copy(
            src_ref=src, dst_ref=dst, send_sem=send, recv_sem=recv, device_id=device, device_id_type=MESH
        )

    loads = [
        pltpu.make_async_copy(src, dst, load_sem.at[i])
        for i, (src, dst) in enumerate(
            [(rows_in, rows_v), (lens_in, lens_s), (win, win_v), (wout, wout_v)]
        )
    ]
    for load in loads:
        load.start()
    tokens = hid_v.shape[0] // CHUNKS
    chunk_loads = []
    for i in range(CHUNKS):
        at = pl.ds(i * tokens, tokens)
        chunk_loads.append((
            pltpu.make_async_copy(hid.at[at], hid_v.at[at], hid_sem.at[i]),
            pltpu.make_async_copy(grad.at[at], grad_v.at[at], grad_sem.at[i]),
        ))
    def load_chunks(first, last):
        for pair in chunk_loads[first:last]:
            for load in pair:
                load.start(priority=int(first > 0))

    load_chunks(0, 1)
    load_chunks(1, 4)

    x_peers = [(dp, lax.rem(x + d, NX) * 2 + zh) for d in (1, 2, 3)]
    z_peer = (dp, x * 2 + 1 - zh)
    y_peers = [(zl * 8 + lax.rem(y + d, NY) * 2 + core, tn) for d in (1, 2, 3)]
    core_peer = (zl * 8 + y * 2 + 1 - core, tn)
    q_y = (y % 2) * 2 + zh
    q_targets = [((x % 2 + z) * 8 + q_y * 2 + 1 - core, zl * 2 + y // 2) for z in (0, 2)]
    q_sources = [(x * 8 + (zh * 2 + y // 2) * 2 + 1 - core, (zl % 2 + z) * 2 + y % 2) for z in (0, 2)]
    q_partner = ((zl + 1 - 2 * (zl % 2)) * 8 + y * 2 + core, tn)
    row_sources = [
        (z * 8 + lax.rem(x - y - zl - z + 3 * NY, NY) * 2 + core, x * 2 + (zh + crossed(z, zl)) % 2) for z in range(NZ)
    ]
    row_peers = [
        (zl * 8 + lax.rem(y + d, NY) * 2 + core, lax.rem(x + d, NX) * 2 + zh) for d in (1, 2, 3)
    ]
    self_row = x == 2 * ((zl + y) % 2)
    barrier = pltpu.get_barrier_semaphore()

    def signal(sem, devices):
        for device in devices:
            pl.semaphore_signal(sem, inc=1, device_id=device, device_id_type=MESH)

    signal(barrier, [z_peer, *q_sources, q_partner])
    for z, device in enumerate(row_sources):

        @pl.when(jnp.logical_not(self_row & (z == zl)))
        def _(device=device):
            signal(barrier, [device])

    load_chunks(4, 6)
    signal(barrier, [*x_peers, *y_peers, core_peer, *row_peers])
    load_chunks(6, CHUNKS)
    sig_copy = pltpu.make_async_copy(sigma_v, sigma_s, sig_sem)
    loads[1].wait()
    for load in loads[2:]:
        load.wait()
    wide_in[...] = jnp.concatenate([win_v[...], jnp.zeros_like(win_v)], axis=0).T
    wide_out[...] = jnp.concatenate([jnp.zeros_like(wout_v), wout_v[...]], axis=0).T

    q_pos = (x % 2) * 2 + x // 2
    q_copies = [
        remote(queries, qall.at[1 - core, q_y, q_pos], qs_sem.at[z], qr_sem.at[x // 2], device)
        for z, device in enumerate(q_targets)
    ]
    def ring(at, size):
        return jnp.minimum(at, size - at)

    hops = ring(x, NX) + ring(y, NY) + ring(zh * NZ + zl, 2 * NZ)
    turns = [hops >= CUTS[0], (hops < CUTS[0]) & (hops >= CUTS[1]), hops < CUTS[1]]
    position = lax.broadcasted_iota(jnp.int32, (LEN, 2 * R), 0)
    for i in range(CHUNKS):
        at = pl.ds(i * tokens, tokens)
        for load in chunk_loads[i]:
            load.wait()
        out = jnp.dot(hid_v[at, :], wide_in[...], preferred_element_type=jnp.float32)
        out += jnp.dot(grad_v[at, :], wide_out[...], preferred_element_type=jnp.float32)
        for j in range(tokens // LEN):
            s = i * (tokens // LEN) + j
            block = jnp.where(position < lens_s[s], out[j * LEN : (j + 1) * LEN], 0.0)
            part[s] = block
            coded[s], scale[s : s + 1, :] = quantize(block)
        if i == 2:
            loads[0].wait()
            sigma_v[...] = jnp.broadcast_to(own_order(rows_v[...], dp), sigma_v.shape)
            sig_copy.start()
        for turn, here in enumerate(turns):
            if i == GREET[turn]:

                @pl.when(here)
                def _():
                    pl.semaphore_wait(barrier, 18 - self_row.astype(jnp.int32))
                    signal(known_sem.at[0], row_peers)
                    for copy in q_copies:
                        copy.start()

    sig_copy.wait()

    def store_z(k):
        return lax.rem(zl + FAR_FIRST[k], NZ)

    def store_block(xx, k, h):
        z = store_z(k)
        return z * 8 + lax.rem(xx - y - zl - z + 3 * NY, NY) * 2 + (core + h) % 2

    def source(xx, k, h):
        return sigma_s[store_block(xx, k, h), 0]

    x_copies, xc_copies = {}, []
    for k in range(STEPS):
        for d in (2, 1, 3):
            for h in range(2):
                xsend[d - 1, k, h] = coded[source(lax.rem(x + d, NX), k, h)]
            n = (d - 1) * STEPS + k
            copy = remote(xsend.at[d - 1, k], xrecv.at[d - 1, k], xs_sem.at[n], xr_sem.at[n], x_peers[d - 1])
            copy.start()
            x_copies[k, d] = copy
        for d in (2, 1, 3) if k == 0 else ():
            for kk in range(STEPS):
                for h in range(2):
                    s = source(lax.rem(x + d, NX), kk, h)
                    xsscale[d - 1, 2 * kk + h : 2 * kk + h + 1, :] = scale[pl.ds(s, 1), :]
            copy = remote(
                xsscale.at[d - 1], xrscale.at[d - 1], xcs_sem.at[d - 1], xcr_sem.at[d - 1], x_peers[d - 1]
            )
            copy.start()
            xc_copies.append(copy)

    for copy in xc_copies:
        copy.wait_recv()
    z_copies, zc_copies, b_copies = [], [], []

    def z_step(k):
        for d in (2, 1, 3):
            x_copies[k, d].wait_recv()
        for h in range(2):
            total = part[source(x, k, h)]
            for d in (1, 2, 3):
                n = 2 * k + h
                total += dequantize(xrecv[d - 1, k, h], xrscale[d - 1, n : n + 1, :])
            zsend[k, h], zsscale[k, h : h + 1, :] = quantize(total)
        z_copies.append(remote(zsend.at[k], zrecv.at[k], zs_sem.at[k], zr_sem.at[k], z_peer))
        z_copies[-1].start()
        zc_copies.append(remote(zsscale.at[k], zrscale.at[k], zcs_sem.at[k], zcr_sem.at[k], z_peer))
        zc_copies[-1].start()

    def b_step(k):
        z_copies[k].wait_recv()
        zc_copies[k].wait_recv()
        for h in range(2):
            total = dequantize(zsend[k, h], zsscale[k, h : h + 1, :])
            total += dequantize(zrecv[k, h], zrscale[k, h : h + 1, :])
            kron = lax.dot_general(
                total[:, :R], total[:, R:], (((0,), (0,)), ((), ())),
                precision=lax.Precision.HIGHEST, preferred_element_type=jnp.float32,
            )
            mean = jnp.sum(jnp.sum(kron * kron, axis=0, keepdims=True), axis=1, keepdims=True) * (1.0 / (R * R))
            normed = kron * (1.0 / jnp.sqrt(mean + 1e-06))
            bsend[2 * k + h] = normed.reshape(R * R // 128, 128).astype(jnp.bfloat16)
        for h in range(2):
            q, near = store_block(x, k, h), (zh + crossed(zl, store_z(k))) % 2
            row = bsend.at[2 * k + h]
            for d in (2, 1, 3, 0):
                n = (2 * k + h) * NX + d
                copy = remote(row, brecv.at[dp], bs_sem.at[n], br_sem, (q, lax.rem(x + d, NX) * 2 + near))
                if FAR_FIRST[k] == 0 and h == 0 and d == 0:

                    @pl.when(self_row)
                    def _(row=row):
                        pltpu.make_async_copy(row, brecv.at[dp], br_sem).start()

                    @pl.when(jnp.logical_not(self_row))
                    def _(copy=copy):
                        copy.start()

                    first_copy.append(copy)
                else:
                    copy.start()
                    b_copies.append(copy)

    first_copy = []
    z_step(0)
    half = qall.at[core, y, pl.ds((zl % 2) * 2, 2)]
    for i in range(2):
        pltpu.make_async_copy(queries, half.at[i], qr_sem.at[i]).wait()
    q_copies.append(remote(half, half, qs_sem.at[11], qr_sem.at[11], q_partner))
    q_copies[-1].start()
    z_step(1)
    pl.semaphore_wait(known_sem.at[0], 3)
    signal(known_sem.at[1], [core_peer])
    z_step(2)
    z_step(3)
    q_copies[2].wait_recv()
    mine = qall.at[core, y]
    for d, device in enumerate(y_peers):
        q_copies.append(remote(mine, mine, qs_sem.at[4 + d], qr_sem.at[4 + d], device))
        q_copies[-1].start()

    def to_core(d):
        block = qall.at[core, lax.rem(y + d, NY)]
        q_copies.append(remote(block, block, qs_sem.at[7 + d], qr_sem.at[7 + d], core_peer))
        q_copies[-1].start()

    to_core(0)
    pl.semaphore_wait(known_sem.at[1], 1)
    for k in range(STEPS):
        b_step(k)
    for d in (1, 3, 2):
        block = qall.at[core, lax.rem(y + d, NY)]
        remote(block, block, qs_sem.at[3 + d], qr_sem.at[7 - d], core_peer).wait_recv()
        to_core(d)

    holder, _, block, row = tables(rows_v[...])
    slot = pick(holder, row, block == dp)
    place = lax.broadcasted_iota(jnp.int32, (DP, SEQ), 1) == slot
    for copy in q_copies[-4:]:
        copy.wait_recv()

    for copy in [*q_copies, *xc_copies, *x_copies.values(), *z_copies, *zc_copies, *b_copies]:
        copy.wait_send()

    @pl.when(jnp.logical_not(self_row))
    def _():
        first_copy[0].wait_send()

    pltpu.make_async_copy(brecv, brecv, br_sem).wait()
    flat[...] = brecv[...].reshape(flat.shape).astype(jnp.float32)
    cols = R * R // 128
    for a in range(cols):
        wide[:, a * 128 : (a + 1) * 128] = flat[pl.ds(a, DP, stride=cols), :].astype(jnp.bfloat16)
    ordered = place.astype(jnp.bfloat16)
    mine = wide[:, pl.ds(pl.multiple_of(tn * QCOLS, QCOLS), QCOLS)]
    store_ref[...] = lax.dot_general(
        ordered, mine, (((0,), (0,)), ((), ())), preferred_element_type=jnp.float32
    ).astype(jnp.bfloat16)
    total = jnp.zeros((DP, 4 * QROWS), jnp.float32)
    for c in range(TP):
        block = jnp.concatenate(
            [qall[1 - m % 2, (m // 2) * 2 + c % 2, (c // 2 % 2) * 2 + c // 4] for m in range(4)], axis=0
        )
        total += lax.dot_general(
            wide[:, c * QCOLS : (c + 1) * QCOLS], block, (((1,), (1,)), ((), ())), preferred_element_type=jnp.float32
        )
    scores_ref[...] = lax.dot_general(
        place.astype(jnp.float32), total, (((0,), (0,)), ((), ())),
        precision=lax.Precision.HIGHEST, preferred_element_type=jnp.float32,
    ) * (1.0 / R)


def hand_over(store_in, scores_in, store_ref, scores_ref):
    store_ref[...] = store_in[...]
    scores_ref[...] = scores_in[...]


def per_device(hidden_in, grad_out, proj_in, proj_out, lengths, store_row, queries):
    rows = store_row.reshape(-1, 128)
    dma, vmem = pltpu.SemaphoreType.DMA, pltpu.VMEM
    bf16, f32, i16, i32 = jnp.bfloat16, jnp.float32, jnp.int16, jnp.int32
    tokens, wide_k = hidden_in.shape
    narrow_k = grad_out.shape[1]
    results = pl.pallas_call(
        kernel,
        out_shape=(
            jax.ShapeDtypeStruct((SEQ, QCOLS), bf16),
            jax.ShapeDtypeStruct((SEQ, 4 * QROWS), f32),
        ),
        in_specs=[pl.BlockSpec(memory_space=pltpu.HBM)] * 7,
        out_specs=(pl.BlockSpec(memory_space=pltpu.VMEM),) * 2,
        scratch_shapes=[
            vmem((tokens, wide_k), bf16), vmem((tokens, narrow_k), bf16),
            vmem((R, wide_k), bf16), vmem((R, narrow_k), bf16),
            vmem((wide_k, 2 * R), bf16), vmem((narrow_k, 2 * R), bf16),
            pltpu.SMEM((SEQ,), i32), vmem(rows.shape, i32),
            vmem((DP, 128), i32), pltpu.SMEM((DP, 128), i32),
            vmem((SEQ, LEN, 2 * R), f32), vmem((SEQ, LEN, 2 * R), i16), vmem((SEQ, 2 * R), f32),
            vmem((3, STEPS, 2, LEN, 2 * R), i16), vmem((3, 2 * STEPS, 2 * R), f32),
            vmem((3, STEPS, 2, LEN, 2 * R), i16), vmem((3, 2 * STEPS, 2 * R), f32),
            vmem((STEPS, 2, LEN, 2 * R), i16), vmem((STEPS, 2, 2 * R), f32),
            vmem((STEPS, 2, LEN, 2 * R), i16), vmem((STEPS, 2, 2 * R), f32),
            vmem((2 * STEPS, 32, 128), bf16), vmem((DP, 32, 128), bf16),
            vmem((2, NY, NX, QROWS, QCOLS), bf16), vmem((DP * 32, 128), f32), vmem((DP, R * R), bf16),
            dma((4,)), dma((CHUNKS,)), dma((CHUNKS,)), dma,
            dma((3 * STEPS,)), dma((3 * STEPS,)), dma((3,)), dma((3,)),
            dma((STEPS,)), dma((STEPS,)), dma((STEPS,)), dma((STEPS,)),
            dma((2 * STEPS * NX,)), dma, dma((12,)), dma((12,)), pltpu.SemaphoreType.REGULAR((2,)),
        ],
        compiler_params=pltpu.CompilerParams(collective_id=0, has_side_effects=True, vmem_limit_bytes=63 * 2**20),
    )(hidden_in, grad_out, proj_in.T, proj_out.T, lengths, rows, queries)
    whole = pl.BlockSpec(memory_space=vmem)
    return pl.pallas_call(
        hand_over,
        out_shape=tuple(jax.ShapeDtypeStruct(r.shape, r.dtype) for r in results),
        in_specs=[whole] * 2,
        out_specs=(whole,) * 2,
    )(*results)


def solution(mesh):
    placed = (
        P("dp", "tensor"), P("dp", "tensor"), P("tensor", None), P("tensor", None),
        P("dp"), P(), P("dp", "tensor"),
    )
    return jax.shard_map(
        per_device, mesh=mesh, in_specs=placed, out_specs=(P("dp", "tensor"), P("dp", "tensor")), check_vma=False
    )
```
